128 devices in a mesh: var: 32 (over y, z, core), mem: 4 (over x).
Axes of the slice: x: 4, y: 4, z: 4, core: 2. Of those that a mesh axis runs over, the one named last changes fastest.
Arguments:
- ensemble: float32 [80, 2097152], P('mem', 'var'), may hold values from -6 to 6
- ray_cells: int32 [4, 256, 64], replicated, may hold values from 0 to 2097151
- ray_weights: float32 [4, 256, 64], replicated, may hold values from 0.06 to 0.19
- ray_centers: int32 [4, 256], replicated, may hold values from 0 to 127
- obs_values: float32 [4, 256], replicated, may hold values from -6 to 6
- obs_var: float32 [4, 256], replicated, may hold values from 0.25 to 4
Outputs:
- posterior: float32 [80, 2097152], P('mem', 'var')
The draws below stay inside these ranges and needn't reach their ends.
All inputs are finite; a program needn't handle non-finite values.
Results may differ from the reference program's by a relative error of at most 0.00014.
Values sent between devices are 32-bit elements; how exact they have to be, the bound alone decides.
A program may use at most 128 MiB of HBM per device.

```python
import math
import jax
import jax.numpy as jnp
from jax import lax

MEMBERS = 80
CELLS = 16384
NOBS = 256
NBATCH = 4
KCELLS = 64
LRAD = 4
NV = 2097152
N_VAR = 32
N_MEM = 4


def with_ends(values, stream_key, least, largest):
    spot = [jax.random.randint(jax.random.fold_in(stream_key, axis), (), 0, length) for axis, length in enumerate(values.shape)]
    main_axis = values.shape.index(max(values.shape))
    beside = spot[:main_axis] + [(spot[main_axis] + 1) % values.shape[main_axis]] + spot[main_axis + 1:]
    return values.at[tuple(spot)].set(least).at[tuple(beside)].set(largest)


def shard_levels(own_key, extent, cuts, least, largest):
    level, own = 1.0, jax.random.fold_in(own_key, 6)
    for dim, shards_of in cuts:
        draws = jnp.exp(jax.random.uniform(jax.random.fold_in(own, dim), (shards_of,), jnp.float32, least / len(cuts), largest / len(cuts)))
        level = level * jnp.repeat(draws, extent[dim] // shards_of).reshape([-1 if axis == dim else 1 for axis in range(len(extent))])
    return level


def noise(stream_key, shape, width, reach, shards=(), kind=jnp.bfloat16):
    array = jax.random.normal(stream_key, shape, jnp.float32) * width
    if len(shards) > 0:
        array = shard_levels(stream_key, shape, shards, -0.22, 0.18) * array
    return jnp.clip(array, min=-reach, max=reach).astype(kind)


def setup_inputs(seed: int = 0) -> dict:
    keys = jax.random.split(jax.random.key(seed), 7)
    return {
        "ensemble": noise(keys[0], (MEMBERS, NV), 1.0, 6.0, ((0, 4), (1, 32)), jnp.float32),
        "ray_cells": with_ends(jax.random.randint(keys[1], (NBATCH, NOBS, KCELLS), 0, NV), jax.random.fold_in(keys[1], 1), 0, NV - 1).astype(jnp.int32),
        "ray_weights": jnp.clip(jax.random.uniform(keys[2], (NBATCH, NOBS, KCELLS), jnp.float32, 0.06, 0.19), 0.06, 0.19),
        "ray_centers": with_ends(jax.random.randint(keys[3], (NBATCH, NOBS), 0, N_VAR * N_MEM), jax.random.fold_in(keys[3], 1), 0, (N_VAR * N_MEM) - 1).astype(jnp.int32),
        "obs_values": noise(keys[4], (NBATCH, NOBS), 1.5, 6.0, (), jnp.float32),
        "obs_var": jnp.clip(jnp.exp(jax.random.uniform(keys[5], (NBATCH, NOBS), jnp.float32, math.log(0.25), math.log(4.0))), 0.25, 4.0),
    }


HIGHEST_PREC = lax.Precision.HIGHEST
EPSILON = 1e-06

def innovations(prior_ens, obs_now, error_var):
    members = prior_ens.shape[0]
    prior_mean = lax.optimization_barrier(jnp.mean(prior_ens, axis=0))
    anomaly = prior_ens - prior_mean
    variance = lax.optimization_barrier(jnp.sum(anomaly * anomaly, axis=0)) / (members - 1) + EPSILON
    total_var = variance + error_var
    post_mean = (prior_mean * error_var + obs_now * variance) / total_var
    shrink = jnp.sqrt(error_var / total_var)
    increments = post_mean - prior_mean + (shrink - 1.0) * anomaly
    regress = anomaly / ((members - 1) * variance)
    return (increments, regress)

def taper_weights(positions, centers):
    centre_pos = (centers.astype(jnp.float32) + 0.5) * CELLS
    distance = jnp.abs(positions[None, :] - centre_pos[:, None]) / (LRAD * CELLS)
    return jnp.maximum(0.0, 1.0 - distance)

def increment_block(cell_block, positions, increments, regress, centers):
    slopes = jnp.dot(regress.T, cell_block, precision=HIGHEST_PREC)
    slopes = slopes * taper_weights(positions, centers)
    return cell_block + jnp.dot(increments, slopes, precision=HIGHEST_PREC)

def reference(ensemble, ray_cells, ray_weights, ray_centers, obs_values, obs_var):
    members, total_cells = ensemble.shape
    blocks = total_cells // CELLS
    columns = ensemble.reshape(members, blocks, CELLS).transpose(1, 0, 2)
    starts = jnp.arange(blocks, dtype=jnp.int32) * CELLS
    iota_cells = jnp.arange(CELLS, dtype=jnp.int32)
    for batch_index in range(NBATCH):
        indices = ray_cells[batch_index]
        picked = columns[indices // CELLS, :, indices % CELLS]
        prior_ens = jnp.einsum('jkm,jk->mj', picked, ray_weights[batch_index], precision=HIGHEST_PREC)
        increments, regress = innovations(prior_ens, obs_values[batch_index], obs_var[batch_index])
        centers = ray_centers[batch_index]

        def update(item_pair):
            cell_block, block_start = item_pair
            positions = (block_start + iota_cells).astype(jnp.float32)
            return increment_block(cell_block, positions, increments, regress, centers)
        columns = lax.map(update, (columns, starts))
    return columns.transpose(1, 0, 2).reshape(members, total_cells)
```

```python
import functools

import jax
import jax.numpy as jnp
from jax import lax
from jax.experimental import pallas as pl
from jax.experimental.pallas import tpu as pltpu
from jax.sharding import PartitionSpec as P

CELLS = 16384
NBATCH = 4
LRAD = 4
EPSILON = 1e-06
LANES = 128
HIGHEST_PREC = lax.Precision.HIGHEST
MESH = pl.DeviceIdType.MESH
BF16 = jnp.bfloat16
F32 = jnp.float32


def innovations(prior_ens, obs_now, error_var):
    members = prior_ens.shape[0]
    prior_mean = jnp.mean(prior_ens, axis=0)
    anomaly = prior_ens - prior_mean
    variance = jnp.sum(anomaly * anomaly, axis=0) / (members - 1) + EPSILON
    total_var = variance + error_var
    post_mean = (prior_mean * error_var + obs_now * variance) / total_var
    shrink = jnp.sqrt(error_var / total_var)
    increments = post_mean - prior_mean + (shrink - 1.0) * anomaly
    regress = anomaly / ((members - 1) * variance)
    return (increments, regress)


def taper_weights(positions, centers, cells):
    centre_pos = (centers.astype(jnp.float32) + 0.5) * cells
    distance = jnp.abs(positions[None, :] - centre_pos[:, None]) / (LRAD * cells)
    return jnp.maximum(0.0, 1.0 - distance)


def increment_block(cell_block, positions, increments, regress, centers, cells):
    slopes = jnp.dot(regress.T, cell_block, precision=HIGHEST_PREC)
    slopes = slopes * taper_weights(positions, centers, cells)
    return cell_block + jnp.dot(increments, slopes, precision=HIGHEST_PREC)


def plain(ensemble, ray_cells, ray_weights, ray_centers, obs_values, obs_var):
    groups = lax.axis_size("mem")
    cell_count = ensemble.shape[1] // groups
    anchor = (lax.axis_index("var") * groups + lax.axis_index("mem")) * cell_count
    positions = (anchor + jnp.arange(cell_count, dtype=jnp.int32)).astype(jnp.float32)
    columns = lax.all_to_all(ensemble, "mem", split_axis=1, concat_axis=0, tiled=True)
    for batch_index in range(NBATCH):
        offsets = ray_cells[batch_index] - anchor
        inside = (offsets >= 0) & (offsets < cell_count)
        clipped = jnp.clip(offsets, 0, cell_count - 1)
        picked = jnp.take(columns, clipped.reshape(-1), axis=1)
        picked = picked.reshape(columns.shape[0], clipped.shape[0], clipped.shape[1])
        weights_here = jnp.where(inside, ray_weights[batch_index], 0.0)
        partial_ens = jnp.einsum("mjk,jk->mj", picked, weights_here, precision=HIGHEST_PREC)
        prior_ens = lax.psum(partial_ens, ("var", "mem"))
        increments, regress = innovations(prior_ens, obs_values[batch_index], obs_var[batch_index])
        columns = increment_block(columns, positions, increments, regress, ray_centers[batch_index], cell_count)
    return lax.all_to_all(columns, "mem", split_axis=0, concat_axis=1, tiled=True)


def lanes_of(shape):
    return lax.broadcasted_iota(jnp.int32, shape, 1)


def squeeze_rows(packed, weight, mask):
    rows = packed.shape[0]
    lane = lanes_of(packed.shape)
    marks = mask.astype(BF16)
    upper = lax.broadcasted_iota(jnp.int32, (LANES, LANES), 0) < lanes_of((LANES, LANES))
    before = jnp.dot(marks, upper.astype(BF16), preferred_element_type=F32)
    count = jnp.dot(marks, jnp.ones((LANES, LANES), BF16), preferred_element_type=F32).astype(jnp.int32)
    gap = jnp.where(mask, lane - before.astype(jnp.int32), -1)
    for bit in range(7):
        step = 1 << bit
        moved_gap = pltpu.roll(gap, LANES - step, 1)
        take = (moved_gap >= 0) & ((moved_gap & step) != 0)
        keep = (gap >= 0) & ((gap & step) == 0)
        packed = jnp.where(take, pltpu.roll(packed, LANES - step, 1), packed)
        weight = jnp.where(take, pltpu.roll(weight, LANES - step, 1), weight)
        gap = jnp.where(take, moved_gap, jnp.where(keep, gap, -1))
    while rows > 8:
        rows //= 2
        first, second = count[:rows], count[rows:]
        p2, w2 = packed[rows:], weight[rows:]
        for bit in range(7):
            step = 1 << bit
            far = (first & step) != 0
            p2 = jnp.where(far, pltpu.roll(p2, step, 1), p2)
            w2 = jnp.where(far, pltpu.roll(w2, step, 1), w2)
        own = lanes_of(first.shape) < first
        packed = jnp.where(own, packed[:rows], p2)
        weight = jnp.where(own, weight[:rows], w2)
        count = first + second
    return packed, weight, count


def pick_kernel(n_mem, kcells, cells_ref, weights_ref, ens_ref, g_ref, ray_ref, place_ref,
                ens_v, xt, graw, w_v, n_v, list_s, n_s, ens_sem, list_sem):
    members, span = ens_ref.shape
    batch_rows = cells_ref.shape[0] // NBATCH
    load = pltpu.make_async_copy(ens_ref, ens_v, ens_sem)
    load.start()
    base = lax.axis_index("var") * span
    for batch in range(NBATCH):
        rows = pl.ds(batch * batch_rows, batch_rows)
        place = cells_ref[rows, :] - base
        mask = (place >= 0) & (place < span)
        row = lax.broadcasted_iota(jnp.int32, place.shape, 0)
        ray = row * (LANES // kcells) + lanes_of(place.shape) // kcells
        packed, weight, count = squeeze_rows(jnp.bitwise_or(ray << 16, place & 0xFFFF), weights_ref[rows, :], mask)
        valid = lanes_of(count.shape) < count
        out_rows = pl.ds(batch * 8, 8)
        place_ref[out_rows, :] = jnp.where(valid, packed & 0xFFFF, 0)
        ray_ref[out_rows, :] = jnp.where(valid, packed >> 16, -1)
        w_v[out_rows, :] = jnp.where(valid, weight, 0.0)
        n_v[out_rows, :] = count
    to_list = pltpu.make_async_copy(place_ref, list_s, list_sem.at[0])
    to_count = pltpu.make_async_copy(n_v, n_s, list_sem.at[1])
    to_list.start()
    to_count.start()
    load.wait()

    def turn(group, carry):
        tiles = []
        for part in range(4):
            at = pl.ds(pl.multiple_of(group * 4 * LANES + part * LANES, LANES), LANES)
            tiles.append(ens_v[:, at])
            tiles.append(jnp.zeros((32 - members, LANES), F32))
        xt[pl.ds(pl.multiple_of(group * LANES, LANES), LANES), :] = jnp.concatenate(tiles, axis=0).T
        return carry

    lax.fori_loop(0, span // (4 * LANES), turn, 0)
    to_list.wait()
    to_count.wait()

    def gather_row(row, carry):
        def gather_eight(block, inner):
            for unit in range(8):
                slot = block * 8 + unit
                place = list_s[row, slot]
                source = ((place >> 9) << 7) | (place & 127)
                graw[pl.ds(row * LANES + slot, 1), :] = xt[pl.ds(source, 1), :]
            return inner

        lax.fori_loop(0, (n_s[row, 0] + 7) // 8, gather_eight, 0)
        return carry

    lax.fori_loop(0, NBATCH * 8, gather_row, 0)

    per_mem = 8 // n_mem
    for row in range(NBATCH * 8):
        batch, lane_group = row // 8, row % 8
        owner, inner = lane_group // per_mem, lane_group % per_mem
        raw = graw[pl.ds(row * LANES, LANES), :].T
        part = (place_ref[pl.ds(row, 1), :] >> 7) & 3
        total = jnp.zeros((24, LANES), F32)
        for piece in range(4):
            total = jnp.where(part == piece, raw[32 * piece:32 * piece + 24, :], total)
        total = jnp.where(ray_ref[pl.ds(row, 1), :] >= 0, total, 0.0) * w_v[pl.ds(row, 1), :]
        at = ((owner * NBATCH + batch) * per_mem + inner) * LANES
        g_ref[:, pl.ds(at, LANES)] = total


def pick(ensemble, ray_cells, ray_weights, n_mem):
    members, span = ensemble.shape
    kcells = ray_cells.shape[2]
    rows = ray_cells.size // LANES
    chunks = NBATCH * 8
    vmem = pl.BlockSpec(memory_space=pltpu.VMEM)
    return pl.pallas_call(
        functools.partial(pick_kernel, n_mem, kcells),
        out_shape=(
            jax.ShapeDtypeStruct((24, chunks * LANES), F32),
            jax.ShapeDtypeStruct((chunks, LANES), jnp.int32),
            jax.ShapeDtypeStruct((chunks, LANES), jnp.int32),
        ),
        in_specs=[vmem, vmem, pl.BlockSpec(memory_space=pl.ANY)],
        out_specs=(vmem, vmem, vmem),
        scratch_shapes=[
            pltpu.VMEM((members, span), F32),
            pltpu.VMEM((span // 4, LANES), F32),
            pltpu.VMEM((chunks * LANES, LANES), F32),
            pltpu.VMEM((chunks, LANES), F32),
            pltpu.VMEM((chunks, LANES), jnp.int32),
            pltpu.SMEM((chunks, LANES), jnp.int32),
            pltpu.SMEM((chunks, LANES), jnp.int32),
            pltpu.SemaphoreType.DMA,
            pltpu.SemaphoreType.DMA((2,)),
        ],
        compiler_params=pltpu.CompilerParams(vmem_limit_bytes=48 << 20),
        name="pick",
    )(ray_cells.reshape(rows, LANES), ray_weights.reshape(rows, LANES), ensemble)


def high_dot(a, b):
    return jnp.dot(a, b, precision=HIGHEST_PREC, preferred_element_type=F32)


def main_kernel(dims, ens_ref, g_ref, ray_ref, place_ref, par_ref, out_ref,
                xf, res, xr, rsb, xb, agb, part_v, inc_v, reg_v, dpoly, dhi, dlo,
                mini_s, mini_r, fwd_s, fwd_r, own_sem, red_s, red_r, back_s, back_r):
    n_var, n_mem, members, cells, nobs, n_chunk = dims
    group = members // n_mem
    wide = 24 * n_mem
    slots = 8 // n_mem * LANES
    all_slots = NBATCH * slots
    width = cells // n_chunk
    rays_here = nobs // n_var
    p, q = lax.axis_index("var"), lax.axis_index("mem")

    def var_peer(k):
        return {"var": lax.rem(p + k, n_var)}

    def mem_peer(k):
        return {"mem": lax.rem(q + k, n_mem)}

    barrier = pltpu.get_barrier_semaphore()

    def greet(k, carry):
        pl.semaphore_signal(barrier, inc=1, device_id=var_peer(k), device_id_type=MESH)
        return carry

    lax.fori_loop(1, n_var, greet, 0)
    for k in range(1, n_mem):
        pl.semaphore_signal(barrier, inc=1, device_id=mem_peer(k), device_id_type=MESH)
    pl.semaphore_wait(barrier, n_var - 1 + n_mem - 1)

    mini = []
    for k in range(1, n_mem):
        there = lax.rem(q + k, n_mem)
        copy = pltpu.make_async_remote_copy(
            src_ref=g_ref.at[:, pl.ds(pl.multiple_of(there * all_slots, LANES), all_slots)],
            dst_ref=xr.at[q],
            send_sem=mini_s.at[k], recv_sem=mini_r.at[k],
            device_id=mem_peer(k), device_id_type=MESH)
        copy.start()
        mini.append(copy)
    own = pltpu.make_async_copy(ens_ref.at[:, pl.ds(pl.multiple_of(q * cells, LANES), cells)], xf.at[q], own_sem.at[0])
    own.start()

    def forward(k, chunk):
        there = lax.rem(q + k, n_mem)
        return pltpu.make_async_remote_copy(
            src_ref=ens_ref.at[:, pl.ds(pl.multiple_of(there * cells + chunk * width, LANES), width)],
            dst_ref=xf.at[q, :, pl.ds(pl.multiple_of(chunk * width, LANES), width)],
            send_sem=fwd_s.at[k, chunk], recv_sem=fwd_r.at[k, chunk],
            device_id=mem_peer(k), device_id_type=MESH)

    def start_forward(chunk, carry):
        for k in (2, 1, 3):
            forward(k, chunk).start()
        return carry

    lax.fori_loop(0, n_chunk, start_forward, 0)

    xr[q] = g_ref[:, pl.ds(pl.multiple_of(q * all_slots, LANES), all_slots)]
    lane = lanes_of((1, LANES))
    real_lane = (lax.rem(lane, 24) < group) & (lane < wide)
    block = p * n_mem + q
    per_mem = 8 // n_mem

    def meta_row(ref, batch):
        rows = [ref[pl.ds(batch * 8 + q * per_mem + inner, 1), :] for inner in range(per_mem)]
        return jnp.concatenate(rows, axis=1)

    ray_rows = [meta_row(ray_ref, b) for b in range(NBATCH)]
    pos_rows = [(meta_row(place_ref, b) + p * (n_mem * cells)).astype(F32) for b in range(NBATCH)]
    ray_column = lax.broadcasted_iota(jnp.int32, (nobs, 1), 0)
    part_v[...] = jnp.zeros_like(part_v)
    for copy in mini:
        copy.wait()

    def own_rows():
        return pl.ds(pl.multiple_of(p * rays_here, rays_here), rays_here)

    def start_reduce(batch):
        state = xr[:, :, pl.ds(batch * slots, slots)].reshape(wide, slots)
        chosen = (ray_rows[batch] == ray_column).astype(F32)
        part_v[batch, :, pl.ds(0, wide)] = high_dot(chosen, state.T)

        def send(k, carry):
            there = lax.rem(p + k, n_var)
            pltpu.make_async_remote_copy(
                src_ref=part_v.at[batch, pl.ds(pl.multiple_of(there * rays_here, rays_here), rays_here)],
                dst_ref=rsb.at[batch, p],
                send_sem=red_s.at[batch, 0], recv_sem=red_r.at[batch, 0],
                device_id=var_peer(k), device_id_type=MESH).start()
            return carry

        lax.fori_loop(1, n_var, send, 0)
        rsb[batch, p] = part_v[batch, own_rows(), :]

    def finish_reduce(batch):
        landed = rsb.at[batch, pl.ds(0, n_var - 1)]
        pltpu.make_async_remote_copy(
            src_ref=landed, dst_ref=landed, send_sem=red_s.at[batch, 0], recv_sem=red_r.at[batch, 0],
            device_id=var_peer(1), device_id_type=MESH).wait()
        xb[batch, q] = jnp.sum(rsb[batch], axis=0)
        across = []
        for k in range(1, n_mem):
            copy = pltpu.make_async_remote_copy(
                src_ref=xb.at[batch, q], dst_ref=xb.at[batch, q],
                send_sem=red_s.at[batch, k], recv_sem=red_r.at[batch, k],
                device_id=mem_peer(k), device_id_type=MESH)
            copy.start()
            across.append(copy)
        for copy in across:
            copy.wait()
        agb[batch, own_rows(), :] = jnp.sum(xb[batch], axis=0)
        mine = agb.at[batch, own_rows()]

        def send(k, carry):
            pltpu.make_async_remote_copy(
                src_ref=mine, dst_ref=mine,
                send_sem=red_s.at[batch, n_mem], recv_sem=red_r.at[batch, n_mem],
                device_id=var_peer(k), device_id_type=MESH).start()
            return carry

        lax.fori_loop(1, n_var, send, 0)
        landed = agb.at[batch, pl.ds(0, nobs - rays_here)]
        pltpu.make_async_remote_copy(
            src_ref=landed, dst_ref=landed, send_sem=red_s.at[batch, n_mem], recv_sem=red_r.at[batch, n_mem],
            device_id=var_peer(1), device_id_type=MESH).wait()

    def innovate(batch):
        prior = agb[batch]
        obs = par_ref[:, NBATCH + batch:NBATCH + batch + 1]
        error_var = par_ref[:, 2 * NBATCH + batch:2 * NBATCH + batch + 1]
        mean = jnp.sum(prior, axis=1, keepdims=True) / members
        anomaly = jnp.where(real_lane, prior - mean, 0.0)
        variance = jnp.sum(anomaly * anomaly, axis=1, keepdims=True) / (members - 1) + EPSILON
        total_var = variance + error_var
        post_mean = (mean * error_var + obs * variance) / total_var
        shrink = jnp.sqrt(error_var / total_var)
        increments = jnp.where(real_lane, post_mean - mean + (shrink - 1.0) * anomaly, 0.0)
        inc_v[...] = increments.T
        reg_v[...] = anomaly / ((members - 1) * variance)

    def centre_pos(batch):
        return (par_ref[:, batch:batch + 1] + 0.5) * cells

    def taper_at(batch, positions):
        return 1.0 - jnp.abs(positions - centre_pos(batch)) / (LRAD * cells)

    def update_mini(batch):
        for later in range(batch + 1, NBATCH):
            at = pl.ds(later * slots, slots)
            state = xr[:, :, at].reshape(wide, slots)
            slopes = high_dot(reg_v[:, 0:wide], state)
            slopes = slopes * jnp.maximum(taper_at(batch, pos_rows[later]), 0.0)
            state = state + high_dot(inc_v[0:wide, :], slopes)
            xr[:, :, at] = state.reshape(n_mem, 24, slots)

    def compose(batch):
        for half in range(2):
            start = (block * cells + half * (cells // 2)).astype(F32)
            near, far = taper_at(batch, start), taper_at(batch, start + cells // 2)
            inside = near + far > 0.0
            alpha = jnp.where(inside, near, 0.0)
            beta = jnp.where(inside, far - near, 0.0)
            regress = reg_v[...]
            both = jnp.concatenate([regress * alpha, regress * beta], axis=1)
            ab = high_dot(inc_v[0:wide, :], both)
            a, b = ab[:, :LANES], ab[:, LANES:]
            if batch == 0:
                dpoly[half, 0], dpoly[half, 1] = a, b
                continue
            old = jnp.concatenate([dpoly[half, k] for k in range(batch + 1)], axis=1)
            left = jnp.concatenate([a[:, 0:wide], b[:, 0:wide]], axis=0)
            made = high_dot(left, old)
            for k in range(batch + 2):
                total = a if k == 0 else b if k == 1 else jnp.zeros_like(a)
                if k <= batch:
                    total = total + dpoly[half, k] + made[:wide, k * LANES:(k + 1) * LANES]
                if k >= 1:
                    total = total + made[wide:, (k - 1) * LANES:k * LANES]
                dpoly[half, k] = total

    start_reduce(0)
    for batch in range(NBATCH):
        finish_reduce(batch)
        innovate(batch)
        update_mini(batch)
        if batch + 1 < NBATCH:
            start_reduce(batch + 1)
        compose(batch)

    terms = NBATCH + 1
    for half in range(2):
        for k in range(terms):
            value = dpoly[half, k][:, 0:wide]
            high = value.astype(BF16)
            dhi[half, pl.ds(k * wide, wide), :] = high
            dlo[half, pl.ds(k * wide, wide), :] = (value - high.astype(F32)).astype(BF16)

    own.wait()

    def back(k, chunk):
        there = lax.rem(q + k, n_mem)
        return pltpu.make_async_remote_copy(
            src_ref=res.at[there, :, pl.ds(pl.multiple_of(chunk * width, LANES), width)],
            dst_ref=out_ref.at[:, pl.ds(pl.multiple_of(q * cells + chunk * width, LANES), width)],
            send_sem=back_s.at[k], recv_sem=back_r.at[k],
            device_id=mem_peer(k), device_id_type=MESH)

    pad = jnp.zeros((24 - group, width), F32)

    def apply(chunk, carry):
        for k in (2, 1, 3):
            forward(k, chunk).wait()
        half = chunk // (n_chunk // 2)
        at = pl.ds(pl.multiple_of(chunk * width, LANES), width)
        pieces = []
        for i in range(n_mem):
            pieces += [xf[i, :, at], pad]
        x = jnp.concatenate(pieces, axis=0)
        high = x.astype(BF16)
        low = (x - high.astype(F32)).astype(BF16)
        big, small = dhi[half], dlo[half]
        y = jnp.dot(big, high, preferred_element_type=F32)
        y = y + jnp.dot(big, low, preferred_element_type=F32)
        y = y + jnp.dot(small, high, preferred_element_type=F32)
        t = (lanes_of((1, width)) + (chunk - half * (n_chunk // 2)) * width).astype(F32) * (2.0 / cells)
        total = y[(terms - 1) * wide:]
        for k in range(terms - 2, -1, -1):
            total = y[k * wide:(k + 1) * wide] + t * total
        total = x + total
        for i in range(n_mem):
            res[i, :, at] = total[24 * i:24 * i + group]
        for k in (2, 1, 3):
            back(k, chunk).start()
        return carry

    lax.fori_loop(0, n_chunk, apply, 0)
    mine = pl.ds(pl.multiple_of(q * cells, LANES), cells)
    keep = pltpu.make_async_copy(res.at[q], out_ref.at[:, mine], own_sem.at[1])
    keep.start()
    for k in range(1, n_mem):
        source = lax.rem(q + n_mem - k, n_mem)
        landed = out_ref.at[:, pl.ds(pl.multiple_of(source * cells, LANES), cells)]
        pltpu.make_async_remote_copy(
            src_ref=res.at[lax.rem(q + k, n_mem)], dst_ref=landed, send_sem=back_s.at[k], recv_sem=back_r.at[k],
            device_id=mem_peer(k), device_id_type=MESH).wait()
    keep.wait()


def assimilate(ensemble, picked, rays, places, params, n_var, n_mem):
    group, span = ensemble.shape
    cells = span // n_mem
    nobs = params.shape[0]
    n_chunk = min(16, cells // 256)
    wide = 24 * n_mem
    all_slots = NBATCH * 8 // n_mem * LANES
    vmem = pl.BlockSpec(memory_space=pltpu.VMEM)
    anywhere = pl.BlockSpec(memory_space=pl.ANY)
    dma = pltpu.SemaphoreType.DMA
    dims = (n_var, n_mem, group * n_mem, cells, nobs, n_chunk)
    return pl.pallas_call(
        functools.partial(main_kernel, dims),
        out_shape=jax.ShapeDtypeStruct((group, span), F32),
        in_specs=[anywhere, vmem, vmem, vmem, vmem],
        out_specs=anywhere,
        scratch_shapes=[
            pltpu.VMEM((n_mem, group, cells), F32),
            pltpu.VMEM((n_mem, group, cells), F32),
            pltpu.VMEM((n_mem, 24, all_slots), F32),
            pltpu.VMEM((NBATCH, n_var, nobs // n_var, LANES), F32),
            pltpu.VMEM((NBATCH, n_mem, nobs // n_var, LANES), F32),
            pltpu.VMEM((NBATCH, nobs, LANES), F32),
            pltpu.VMEM((NBATCH, nobs, LANES), F32),
            pltpu.VMEM((LANES, nobs), F32),
            pltpu.VMEM((nobs, LANES), F32),
            pltpu.VMEM((2, NBATCH + 1, wide, LANES), F32),
            pltpu.VMEM((2, (NBATCH + 1) * wide, wide), BF16),
            pltpu.VMEM((2, (NBATCH + 1) * wide, wide), BF16),
            dma((n_mem,)), dma((n_mem,)),
            dma((n_mem, n_chunk)), dma((n_mem, n_chunk)),
            dma((2,)),
            dma((NBATCH, n_mem + 1)), dma((NBATCH, n_mem + 1)),
            dma((n_mem,)), dma((n_mem,)),
        ],
        compiler_params=pltpu.CompilerParams(collective_id=1, has_side_effects=True, vmem_limit_bytes=48 << 20),
        name="assimilate",
    )(ensemble, picked, rays, places, params)


def fast(ensemble, ray_cells, ray_weights, ray_centers, obs_values, obs_var):
    n_var, n_mem = lax.axis_size("var"), lax.axis_size("mem")
    picked, rays, places = pick(ensemble, ray_cells, ray_weights, n_mem)
    params = jnp.concatenate([ray_centers.astype(F32), obs_values, obs_var], axis=0).T
    return assimilate(ensemble, picked, rays, places, params, n_var, n_mem)


def fits(ray_cells, span, n_var):
    owner = ray_cells.reshape(NBATCH, -1, 8, LANES) // span
    hits = owner[..., None] == jnp.arange(n_var, dtype=jnp.int32)
    return jnp.max(jnp.sum(hits.astype(jnp.int32), axis=(1, 3))) <= LANES


def shards(*arrays):
    room = fits(arrays[1], arrays[0].shape[1], lax.axis_size("var"))
    return lax.cond(room, fast, plain, *arrays)


def solution(mesh):
    placed = (P("mem", "var"), P(), P(), P(), P(), P())
    return jax.shard_map(
        shards, mesh=mesh, in_specs=placed, out_specs=P("mem", "var"), check_vma=False
    )
```

```python
import functools

import jax
import jax.numpy as jnp
from jax import lax
from jax.experimental import pallas as pl
from jax.experimental.pallas import tpu as pltpu
from jax.sharding import PartitionSpec as P

CELLS = 16384
NBATCH = 4
LRAD = 4
EPSILON = 1e-06
LANES = 128
HIGHEST_PREC = lax.Precision.HIGHEST
MESH = pl.DeviceIdType.MESH
N_CHUNK = 16
PACE = (2, 1, 2)
BF16 = jnp.bfloat16
F32 = jnp.float32


def innovations(prior_ens, obs_now, error_var):
    members = prior_ens.shape[0]
    prior_mean = jnp.mean(prior_ens, axis=0)
    anomaly = prior_ens - prior_mean
    variance = jnp.sum(anomaly * anomaly, axis=0) / (members - 1) + EPSILON
    total_var = variance + error_var
    post_mean = (prior_mean * error_var + obs_now * variance) / total_var
    shrink = jnp.sqrt(error_var / total_var)
    increments = post_mean - prior_mean + (shrink - 1.0) * anomaly
    regress = anomaly / ((members - 1) * variance)
    return (increments, regress)


def taper_weights(positions, centers, cells):
    centre_pos = (centers.astype(jnp.float32) + 0.5) * cells
    distance = jnp.abs(positions[None, :] - centre_pos[:, None]) / (LRAD * cells)
    return jnp.maximum(0.0, 1.0 - distance)


def increment_block(cell_block, positions, increments, regress, centers, cells):
    slopes = jnp.dot(regress.T, cell_block, precision=HIGHEST_PREC)
    slopes = slopes * taper_weights(positions, centers, cells)
    return cell_block + jnp.dot(increments, slopes, precision=HIGHEST_PREC)


def sum_everywhere(partial_ens):
    axes = ("var", "mem")
    count = lax.axis_size("var") * lax.axis_size("mem")
    members, rays = partial_ens.shape
    pieces = partial_ens.reshape(members, count, rays // count).transpose(1, 0, 2)
    total = jnp.sum(lax.all_to_all(pieces, axes, split_axis=0, concat_axis=0, tiled=True), axis=0)
    copies = jnp.broadcast_to(total, pieces.shape)
    whole = lax.all_to_all(copies, axes, split_axis=0, concat_axis=0, tiled=True)
    return whole.transpose(1, 0, 2).reshape(members, rays)


def plain(ensemble, ray_cells, ray_weights, ray_centers, obs_values, obs_var):
    groups = lax.axis_size("mem")
    cell_count = ensemble.shape[1] // groups
    anchor = (lax.axis_index("var") * groups + lax.axis_index("mem")) * cell_count
    positions = (anchor + jnp.arange(cell_count, dtype=jnp.int32)).astype(jnp.float32)
    columns = lax.all_to_all(ensemble, "mem", split_axis=1, concat_axis=0, tiled=True)
    for batch_index in range(NBATCH):
        offsets = ray_cells[batch_index] - anchor
        inside = (offsets >= 0) & (offsets < cell_count)
        clipped = jnp.clip(offsets, 0, cell_count - 1)
        picked = jnp.take(columns, clipped.reshape(-1), axis=1)
        picked = picked.reshape(columns.shape[0], clipped.shape[0], clipped.shape[1])
        weights_here = jnp.where(inside, ray_weights[batch_index], 0.0)
        partial_ens = jnp.einsum("mjk,jk->mj", picked, weights_here, precision=HIGHEST_PREC)
        prior_ens = sum_everywhere(partial_ens)
        increments, regress = innovations(prior_ens, obs_values[batch_index], obs_var[batch_index])
        columns = increment_block(columns, positions, increments, regress, ray_centers[batch_index], cell_count)
    return lax.all_to_all(columns, "mem", split_axis=0, concat_axis=1, tiled=True)


def lanes_of(shape):
    return lax.broadcasted_iota(jnp.int32, shape, 1)


def squeeze_rows(packed, weight, mask):
    rows = packed.shape[0]
    lane = lanes_of(packed.shape)
    marks = mask.astype(BF16)
    upper = lax.broadcasted_iota(jnp.int32, (LANES, LANES), 0) < lanes_of((LANES, LANES))
    before = jnp.dot(marks, upper.astype(BF16), preferred_element_type=F32)
    count = jnp.dot(marks, jnp.ones((LANES, LANES), BF16), preferred_element_type=F32).astype(jnp.int32)
    gap = jnp.where(mask, lane - before.astype(jnp.int32), -1)
    for bit in range(7):
        step = 1 << bit
        moved_gap = pltpu.roll(gap, LANES - step, 1)
        take = (moved_gap >= 0) & ((moved_gap & step) != 0)
        keep = (gap >= 0) & ((gap & step) == 0)
        packed = jnp.where(take, pltpu.roll(packed, LANES - step, 1), packed)
        weight = jnp.where(take, pltpu.roll(weight, LANES - step, 1), weight)
        gap = jnp.where(take, moved_gap, jnp.where(keep, gap, -1))
    while rows > 8:
        rows //= 2
        first, second = count[:rows], count[rows:]
        p2, w2 = packed[rows:], weight[rows:]
        for bit in range(7):
            step = 1 << bit
            far = (first & step) != 0
            p2 = jnp.where(far, pltpu.roll(p2, step, 1), p2)
            w2 = jnp.where(far, pltpu.roll(w2, step, 1), w2)
        own = lanes_of(first.shape) < first
        packed = jnp.where(own, packed[:rows], p2)
        weight = jnp.where(own, weight[:rows], w2)
        count = first + second
    return packed, weight, count


def pick_kernel(n_var, kcells, cells_ref, weights_ref, ens_ref, g_ref,
                ens_v, xt, graw, id_v, place_v, w_v, n_v, list_s, n_s, ens_sem, list_sem):
    members, span = ens_ref.shape
    batch_rows = cells_ref.shape[0] // NBATCH
    parts = n_var // 8
    part_rows = batch_rows // parts
    rays_here = batch_rows * LANES // kcells // n_var
    load = pltpu.make_async_copy(ens_ref, ens_v, ens_sem)
    load.start()
    base = lax.axis_index("var") * span
    for part in range(parts):
        packs, weights = [], []
        for batch in range(NBATCH):
            rows = pl.ds(batch * batch_rows + part * part_rows, part_rows)
            place = cells_ref[rows, :] - base
            inside = (place >= 0) & (place < span)
            row = lax.broadcasted_iota(jnp.int32, place.shape, 0)
            ray = batch * rays_here + (row >> 3) * (LANES // kcells) + lanes_of(place.shape) // kcells
            packs.append(jnp.where(inside, jnp.bitwise_or(ray << 16, place & 0xFFFF), -1))
            weights.append(weights_ref[rows, :])
        packed = jnp.concatenate(packs, axis=0)
        packed, weight, count = squeeze_rows(packed, jnp.concatenate(weights, axis=0), packed >= 0)
        valid = lanes_of(count.shape) < count
        out_rows = pl.ds(part * 8, 8)
        place_v[out_rows, :] = jnp.where(valid, packed & 0xFFFF, 0)
        id_v[out_rows, :] = jnp.where(valid, packed >> 16, -1)
        w_v[out_rows, :] = jnp.where(valid, weight, 0.0)
        n_v[out_rows, :] = count
    to_list = pltpu.make_async_copy(place_v, list_s, list_sem.at[0])
    to_count = pltpu.make_async_copy(n_v, n_s, list_sem.at[1])
    to_list.start()
    to_count.start()
    load.wait()
    blank = jnp.zeros((32 - members, LANES), F32)

    def turn(step, carry):
        for group in range(4):
            tiles = []
            for part in range(4):
                at = pl.ds(pl.multiple_of(((step * 4 + group) * 4 + part) * LANES, LANES), LANES)
                tiles += [ens_v[:, at], blank]
            to = pl.ds(pl.multiple_of((step * 4 + group) * LANES, LANES), LANES)
            xt[to, :] = jnp.concatenate(tiles, axis=0).T
        return carry

    lax.fori_loop(0, span // (16 * LANES), turn, 0)
    to_list.wait()
    to_count.wait()

    def gather_row(row, carry):
        def gather_some(block, inner):
            found = []
            for unit in range(16):
                place = list_s[row, block * 16 + unit]
                source = ((place >> 9) << 7) | (place & 127)
                found.append(xt[pl.ds(source, 1), :])
            for unit in range(16):
                graw[pl.ds(row * LANES + block * 16 + unit, 1), :] = found[unit]
            return inner

        lax.fori_loop(0, (jnp.minimum(n_s[row, 0], LANES) + 15) // 16, gather_some, 0)
        return carry

    lax.fori_loop(0, n_var, gather_row, 0)
    sub = lax.broadcasted_iota(jnp.int32, (24, LANES), 0)
    for row in range(n_var):
        raw = graw[pl.ds(row * LANES, LANES), :].T
        place = place_v[pl.ds(row, 1), :]
        ids = id_v[pl.ds(row, 1), :]
        quarter = (place >> 7) & 3
        total = jnp.zeros((24, LANES), F32)
        for piece in range(4):
            total = jnp.where(quarter == piece, raw[32 * piece:32 * piece + 24, :], total)
        total = jnp.where(ids >= 0, total, 0.0) * w_v[pl.ds(row, 1), :]
        total = jnp.where(sub == members, ids.astype(F32), total)
        g_ref[row] = jnp.where(sub == members + 1, place.astype(F32), total)


def pick(ensemble, cell_rows, weight_rows, n_var, kcells):
    members, span = ensemble.shape
    vmem = pl.BlockSpec(memory_space=pltpu.VMEM)
    return pl.pallas_call(
        functools.partial(pick_kernel, n_var, kcells),
        out_shape=jax.ShapeDtypeStruct((n_var, 24, LANES), F32),
        in_specs=[vmem, vmem, pl.BlockSpec(memory_space=pl.ANY)],
        out_specs=vmem,
        scratch_shapes=[
            pltpu.VMEM((members, span), F32),
            pltpu.VMEM((span // 4, LANES), F32),
            pltpu.VMEM((n_var * LANES, LANES), F32),
            pltpu.VMEM((n_var, LANES), jnp.int32),
            pltpu.VMEM((n_var, LANES), jnp.int32),
            pltpu.VMEM((n_var, LANES), F32),
            pltpu.VMEM((n_var, LANES), jnp.int32),
            pltpu.SMEM((n_var, LANES), jnp.int32),
            pltpu.SMEM((n_var, LANES), jnp.int32),
            pltpu.SemaphoreType.DMA,
            pltpu.SemaphoreType.DMA((2,)),
        ],
        compiler_params=pltpu.CompilerParams(vmem_limit_bytes=48 << 20),
        name="pick",
    )(cell_rows, weight_rows, ensemble)


def high_dot(a, b):
    return jnp.dot(a, b, precision=HIGHEST_PREC, preferred_element_type=F32)


def split(x):
    high = x.astype(BF16)
    return high, (x - high.astype(F32)).astype(BF16)


def split_dot(a, b):
    a_high, a_low = split(a)
    b_high, b_low = split(b)
    total = jnp.dot(a_high, b_low, preferred_element_type=F32)
    total = total + jnp.dot(a_low, b_high, preferred_element_type=F32)
    return total + jnp.dot(a_high, b_high, preferred_element_type=F32)


def main_kernel(dims, ens_ref, g_ref, par_ref, out_ref,
                xf, res, xr, state, xb, agb, inc_v, reg_v, dpoly, dhi, dlo,
                mini_s, mini_r, fwd_s, fwd_r, own_sem, red_s, red_r, back_s, back_r):
    n_var, n_mem, members, cells, nobs, n_chunk = dims
    group = members // n_mem
    wide = 24 * n_mem
    sources = n_var // n_mem
    width = cells // n_chunk
    rays_here = nobs // n_var
    p, q = lax.axis_index("var"), lax.axis_index("mem")
    taker = p // sources
    stays = taker == q

    def var_peer(k):
        return {"var": lax.rem(p + k, n_var)}

    def mem_peer(k):
        return {"mem": lax.rem(q + k, n_mem)}

    barrier = pltpu.get_barrier_semaphore()

    def greet(k, carry):
        pl.semaphore_signal(barrier, inc=1, device_id=var_peer(k), device_id_type=MESH)
        return carry

    def greet_sender(k, carry):
        source, part = q * sources + k // n_mem, lax.rem(k, n_mem)

        @pl.when((source != p) | (part != q))
        def _():
            pl.semaphore_signal(barrier, inc=1, device_id={"var": source, "mem": part}, device_id_type=MESH)

        return carry

    lax.fori_loop(0, n_var, greet_sender, 0)
    for k in range(1, n_mem):
        pl.semaphore_signal(barrier, inc=1, device_id=mem_peer(k), device_id_type=MESH)
    lax.fori_loop(1, n_var, greet, 0)
    lane = lanes_of((1, LANES))
    real_lane = (lax.rem(lane, 24) < group) & (lane < wide)
    block = p * n_mem + q
    pl.semaphore_wait(barrier, n_var - 1 + n_mem - 1 + n_var - stays.astype(jnp.int32))

    def send_mini(k, carry):
        there = lax.rem(p + k, n_var)

        @pl.when((k > 0) | jnp.logical_not(stays))
        def _():
            pltpu.make_async_remote_copy(
                src_ref=g_ref.at[there], dst_ref=xr.at[q, lax.rem(p, sources)],
                send_sem=mini_s, recv_sem=mini_r,
                device_id={"var": there, "mem": taker}, device_id_type=MESH).start()

        return carry

    lax.fori_loop(0, n_var, send_mini, 0)

    @pl.when(stays)
    def _():
        xr[q, lax.rem(p, sources)] = g_ref[p]

    def forward(k, chunk):
        there = lax.rem(q + k, n_mem)
        return pltpu.make_async_remote_copy(
            src_ref=ens_ref.at[:, pl.ds(pl.multiple_of(there * cells + chunk * width, LANES), width)],
            dst_ref=xf.at[q, :, pl.ds(pl.multiple_of(chunk * width, LANES), width)],
            send_sem=fwd_s.at[k, chunk], recv_sem=fwd_r.at[k, chunk],
            device_id=mem_peer(k), device_id_type=MESH)

    def start_forward(chunk, carry):
        for k in (2, 1, 3):
            forward(k, chunk).start()
        return carry

    paced = [0]

    def pace(count):
        until = min(paced[0] + count, n_chunk)
        lax.fori_loop(paced[0], until, start_forward, 0)
        paced[0] = until

    pace(PACE[0])
    own = pltpu.make_async_copy(ens_ref.at[:, pl.ds(pl.multiple_of(q * cells, LANES), cells)], xf.at[q], own_sem.at[0])
    own.start()

    def wait_mini(count):
        landed = g_ref.at[pl.ds(0, count)]
        pltpu.make_async_remote_copy(
            src_ref=landed, dst_ref=landed, send_sem=mini_s, recv_sem=mini_r,
            device_id=mem_peer(1), device_id_type=MESH).wait()

    @pl.when(stays)
    def _():
        wait_mini(n_var - 1)

    @pl.when(jnp.logical_not(stays))
    def _():
        wait_mini(n_var)

    sub = lax.broadcasted_iota(jnp.int32, (24, LANES), 0)
    ids, places = [], []
    for source in range(sources):
        for part in range(n_mem):
            tile = xr[part, source]
            state[pl.ds(part * 24, 24), pl.ds(source * LANES, LANES)] = jnp.where(sub < group, tile, 0.0)
        ids.append(xr[0, source, group:group + 1, :])
        places.append(xr[0, source, group + 1:group + 2, :] + ((q * sources + source) * (n_mem * cells)).astype(F32))
    id_row = jnp.concatenate(ids, axis=1)
    scale = 1.0 / (LRAD * cells)
    place_row = jnp.concatenate(places, axis=1) * scale
    own_ray = lax.broadcasted_iota(jnp.int32, (rays_here, 1), 0).astype(F32)

    def own_rows():
        return pl.ds(pl.multiple_of(p * rays_here, rays_here), rays_here)

    def across(batch, k):
        return pltpu.make_async_remote_copy(
            src_ref=xb.at[batch, q], dst_ref=xb.at[batch, q],
            send_sem=red_s.at[batch, k], recv_sem=red_r.at[batch, k],
            device_id=mem_peer(k), device_id_type=MESH)

    def start_reduce(batch):
        chosen = (id_row == own_ray + batch * rays_here).astype(BF16)
        held = state[...]
        high = held.astype(BF16)
        rest = held - high.astype(F32)
        middle = rest.astype(BF16)
        low = (rest - middle.astype(F32)).astype(BF16)
        total = jnp.zeros((rays_here, wide), F32)
        for piece in (low, middle, high):
            total = total + lax.dot_general(chosen, piece, (((1,), (1,)), ((), ())), preferred_element_type=F32)
        xb[batch, q] = jnp.concatenate([total, jnp.zeros((rays_here, LANES - wide), F32)], axis=1)
        for k in (2, 1, 3):
            across(batch, k).start()

    def finish_reduce(batch):
        for k in (2, 1, 3):
            across(batch, k).wait()
        agb[batch, own_rows(), :] = jnp.sum(xb[batch], axis=0)
        mine = agb.at[batch, own_rows()]

        def send(k, carry):
            pltpu.make_async_remote_copy(
                src_ref=mine, dst_ref=mine,
                send_sem=red_s.at[batch, n_mem], recv_sem=red_r.at[batch, n_mem],
                device_id=var_peer(k), device_id_type=MESH).start()
            return carry

        lax.fori_loop(1, n_var, send, 0)
        pace(PACE[2])
        landed = agb.at[batch, pl.ds(0, nobs - rays_here)]
        pltpu.make_async_remote_copy(
            src_ref=landed, dst_ref=landed, send_sem=red_s.at[batch, n_mem], recv_sem=red_r.at[batch, n_mem],
            device_id=var_peer(1), device_id_type=MESH).wait()

    def innovate(batch):
        prior = agb[batch]
        obs = par_ref[:, NBATCH + batch:NBATCH + batch + 1]
        error_var = par_ref[:, 2 * NBATCH + batch:2 * NBATCH + batch + 1]
        mean = jnp.sum(prior, axis=1, keepdims=True) / members
        anomaly = jnp.where(real_lane, prior - mean, 0.0)
        variance = jnp.sum(anomaly * anomaly, axis=1, keepdims=True) / (members - 1) + EPSILON
        total_var = variance + error_var
        post_mean = (mean * error_var + obs * variance) / total_var
        shrink = jnp.sqrt(error_var / total_var)
        increments = jnp.where(real_lane, post_mean - mean + (shrink - 1.0) * anomaly, 0.0)
        inc_v[...] = increments.T
        reg_v[...] = anomaly / ((members - 1) * variance)

    def taper_at(batch, scaled):
        return 1.0 - jnp.abs(scaled - (par_ref[:, batch:batch + 1] + 0.5) * (cells * scale))

    def update_state(batch):
        slopes = split_dot(reg_v[:, 0:wide], state[...])
        slopes = slopes * jnp.maximum(taper_at(batch, place_row), 0.0)
        state[...] += split_dot(inc_v[0:wide, :], slopes)

    def compose(batch):
        for half in range(2):
            start = (block * cells + half * (cells // 2)).astype(F32) * scale
            near, far = taper_at(batch, start), taper_at(batch, start + (cells // 2) * scale)
            inside = near + far > 0.0
            alpha = jnp.where(inside, near, 0.0)
            beta = jnp.where(inside, far - near, 0.0)
            regress = reg_v[...]
            both = jnp.concatenate([regress * alpha, regress * beta], axis=1)
            ab = high_dot(inc_v[0:wide, :], both)
            a, b = ab[:, :LANES], ab[:, LANES:]
            if batch == 0:
                dpoly[half, 0], dpoly[half, 1] = a, b
                continue
            old = jnp.concatenate([dpoly[half, k] for k in range(batch + 1)], axis=1)
            left = jnp.concatenate([a[:, 0:wide], b[:, 0:wide]], axis=0)
            made = high_dot(left, old)
            for k in range(batch + 2):
                total = a if k == 0 else b if k == 1 else jnp.zeros_like(a)
                if k <= batch:
                    total = total + dpoly[half, k] + made[:wide, k * LANES:(k + 1) * LANES]
                if k >= 1:
                    total = total + made[wide:, (k - 1) * LANES:k * LANES]
                dpoly[half, k] = total

    start_reduce(0)
    for batch in range(NBATCH):
        pace(PACE[1])
        if batch:
            compose(batch - 1)
        finish_reduce(batch)
        innovate(batch)
        if batch + 1 < NBATCH:
            update_state(batch)
            start_reduce(batch + 1)
    pace(n_chunk)
    compose(NBATCH - 1)

    terms = NBATCH + 1
    for half in range(2):
        for k in range(terms):
            high, low = split(dpoly[half, k][:, 0:wide])
            dhi[half, pl.ds(k * wide, wide), :] = high
            dlo[half, pl.ds(k * wide, wide), :] = low

    own.wait()

    def back(k, chunk):
        there = lax.rem(q + k, n_mem)
        return pltpu.make_async_remote_copy(
            src_ref=res.at[there, :, pl.ds(pl.multiple_of(chunk * width, LANES), width)],
            dst_ref=out_ref.at[:, pl.ds(pl.multiple_of(q * cells + chunk * width, LANES), width)],
            send_sem=back_s.at[k], recv_sem=back_r.at[k],
            device_id=mem_peer(k), device_id_type=MESH)

    pad = jnp.zeros((24 - group, width), F32)

    def apply(chunk, carry):
        for k in (2, 1, 3):
            forward(k, chunk).wait()
        half = chunk // (n_chunk // 2)
        at = pl.ds(pl.multiple_of(chunk * width, LANES), width)
        pieces = []
        for i in range(n_mem):
            pieces += [xf[i, :, at], pad]
        x = jnp.concatenate(pieces, axis=0)
        high, low = split(x)
        big, small = dhi[half], dlo[half]
        y = jnp.dot(big, high, preferred_element_type=F32)
        y = y + jnp.dot(big, low, preferred_element_type=F32)
        y = y + jnp.dot(small, high, preferred_element_type=F32)
        t = (lanes_of((1, width)) + (chunk - half * (n_chunk // 2)) * width).astype(F32) * (2.0 / cells)
        total = y[(terms - 1) * wide:]
        for k in range(terms - 2, -1, -1):
            total = y[k * wide:(k + 1) * wide] + t * total
        total = x + total
        for i in range(n_mem):
            res[i, :, at] = total[24 * i:24 * i + group]
        for k in (2, 1, 3):
            back(k, chunk).start()
        return carry

    lax.fori_loop(0, n_chunk, apply, 0)
    mine = pl.ds(pl.multiple_of(q * cells, LANES), cells)
    keep = pltpu.make_async_copy(res.at[q], out_ref.at[:, mine], own_sem.at[1])
    keep.start()
    for k in range(1, n_mem):
        source = lax.rem(q + n_mem - k, n_mem)
        landed = out_ref.at[:, pl.ds(pl.multiple_of(source * cells, LANES), cells)]
        pltpu.make_async_remote_copy(
            src_ref=res.at[lax.rem(q + k, n_mem)], dst_ref=landed, send_sem=back_s.at[k], recv_sem=back_r.at[k],
            device_id=mem_peer(k), device_id_type=MESH).wait()
    keep.wait()


def assimilate(ensemble, picked, params, n_var, n_mem):
    group, span = ensemble.shape
    cells = span // n_mem
    nobs = params.shape[0]
    wide = 24 * n_mem
    slots = n_var // n_mem * LANES
    rays_here = nobs // n_var
    vmem = pl.BlockSpec(memory_space=pltpu.VMEM)
    anywhere = pl.BlockSpec(memory_space=pl.ANY)
    dma = pltpu.SemaphoreType.DMA
    dims = (n_var, n_mem, group * n_mem, cells, nobs, N_CHUNK)
    return pl.pallas_call(
        functools.partial(main_kernel, dims),
        out_shape=jax.ShapeDtypeStruct((group, span), F32),
        in_specs=[anywhere, vmem, vmem],
        out_specs=anywhere,
        scratch_shapes=[
            pltpu.VMEM((n_mem, group, cells), F32),
            pltpu.VMEM((n_mem, group, cells), F32),
            pltpu.VMEM((n_mem, n_var // n_mem, 24, LANES), F32),
            pltpu.VMEM((wide, slots), F32),
            pltpu.VMEM((NBATCH, n_mem, rays_here, LANES), F32),
            pltpu.VMEM((NBATCH, nobs, LANES), F32),
            pltpu.VMEM((LANES, nobs), F32),
            pltpu.VMEM((nobs, LANES), F32),
            pltpu.VMEM((2, NBATCH + 1, wide, LANES), F32),
            pltpu.VMEM((2, (NBATCH + 1) * wide, wide), BF16),
            pltpu.VMEM((2, (NBATCH + 1) * wide, wide), BF16),
            dma, dma,
            dma((n_mem, N_CHUNK)), dma((n_mem, N_CHUNK)),
            dma((2,)),
            dma((NBATCH, n_mem + 1)), dma((NBATCH, n_mem + 1)),
            dma((n_mem,)), dma((n_mem,)),
        ],
        compiler_params=pltpu.CompilerParams(collective_id=1, has_side_effects=True, vmem_limit_bytes=48 << 20),
        name="assimilate",
    )(ensemble, picked, params)


def owner_order(rays, n_var, per_row):
    count = rays.shape[-1] // n_var
    return rays.reshape(-1, n_var // 8, count // per_row, 8, per_row).transpose(0, 1, 3, 2, 4).reshape(rays.shape)


def fast(ensemble, cell_rows, weight_rows, ray_centers, obs_values, obs_var):
    n_var, n_mem = lax.axis_size("var"), lax.axis_size("mem")
    nobs = ray_centers.shape[1]
    kcells = cell_rows.size // (NBATCH * nobs)
    picked = pick(ensemble, cell_rows, weight_rows, n_var, kcells)
    params = jnp.concatenate([ray_centers.astype(F32), obs_values, obs_var], axis=0)
    params = owner_order(params, n_var, LANES // kcells).T
    return assimilate(ensemble, picked, params, n_var, n_mem)


def slow(ensemble, cell_rows, weight_rows, ray_centers, obs_values, obs_var):
    shape = (*ray_centers.shape, cell_rows.size // ray_centers.size)
    return plain(ensemble, cell_rows.reshape(shape), weight_rows.reshape(shape), ray_centers, obs_values, obs_var)


def fits(cell_rows, span, n_var):
    home = cell_rows.reshape(NBATCH, n_var // 8, -1, 8, LANES) // span
    hits = home[..., None] == jnp.arange(n_var, dtype=jnp.int32)
    return jnp.max(jnp.sum(hits.astype(jnp.int32), axis=(0, 2, 4))) <= LANES


def shards(ensemble, ray_cells, ray_weights, *rest):
    cell_rows, weight_rows = ray_cells.reshape(-1, LANES), ray_weights.reshape(-1, LANES)
    room = fits(cell_rows, ensemble.shape[1], lax.axis_size("var"))
    return lax.cond(room, fast, slow, ensemble, cell_rows, weight_rows, *rest)


def solution(mesh):
    placed = (P("mem", "var"), P(), P(), P(), P(), P())
    return jax.shard_map(
        shards, mesh=mesh, in_specs=placed, out_specs=P("mem", "var"), check_vma=False
    )
```

```python
import functools

import jax
import jax.numpy as jnp
from jax import lax
from jax.experimental import pallas as pl
from jax.experimental.pallas import tpu as pltpu
from jax.sharding import PartitionSpec as P

CELLS = 16384
NBATCH = 4
LRAD = 4
EPSILON = 1e-06
LANES = 128
HIGHEST_PREC = lax.Precision.HIGHEST
MESH = pl.DeviceIdType.MESH
N_CHUNK = 16
EARLY = 6
PACE = (2, 1, 1, 0)
BF16 = jnp.bfloat16
F32 = jnp.float32


def innovations(prior_ens, obs_now, error_var):
    members = prior_ens.shape[0]
    prior_mean = jnp.mean(prior_ens, axis=0)
    anomaly = prior_ens - prior_mean
    variance = jnp.sum(anomaly * anomaly, axis=0) / (members - 1) + EPSILON
    total_var = variance + error_var
    post_mean = (prior_mean * error_var + obs_now * variance) / total_var
    shrink = jnp.sqrt(error_var / total_var)
    increments = post_mean - prior_mean + (shrink - 1.0) * anomaly
    regress = anomaly / ((members - 1) * variance)
    return (increments, regress)


def taper_weights(positions, centers, cells):
    centre_pos = (centers.astype(jnp.float32) + 0.5) * cells
    distance = jnp.abs(positions[None, :] - centre_pos[:, None]) / (LRAD * cells)
    return jnp.maximum(0.0, 1.0 - distance)


def increment_block(cell_block, positions, increments, regress, centers, cells):
    slopes = jnp.dot(regress.T, cell_block, precision=HIGHEST_PREC)
    slopes = slopes * taper_weights(positions, centers, cells)
    return cell_block + jnp.dot(increments, slopes, precision=HIGHEST_PREC)


def sum_everywhere(partial_ens):
    axes = ("var", "mem")
    count = lax.axis_size("var") * lax.axis_size("mem")
    members, rays = partial_ens.shape
    pieces = partial_ens.reshape(members, count, rays // count).transpose(1, 0, 2)
    total = jnp.sum(lax.all_to_all(pieces, axes, split_axis=0, concat_axis=0, tiled=True), axis=0)
    copies = jnp.broadcast_to(total, pieces.shape)
    whole = lax.all_to_all(copies, axes, split_axis=0, concat_axis=0, tiled=True)
    return whole.transpose(1, 0, 2).reshape(members, rays)


def plain(ensemble, ray_cells, ray_weights, ray_centers, obs_values, obs_var):
    groups = lax.axis_size("mem")
    cell_count = ensemble.shape[1] // groups
    anchor = (lax.axis_index("var") * groups + lax.axis_index("mem")) * cell_count
    positions = (anchor + jnp.arange(cell_count, dtype=jnp.int32)).astype(jnp.float32)
    columns = lax.all_to_all(ensemble, "mem", split_axis=1, concat_axis=0, tiled=True)
    for batch_index in range(NBATCH):
        offsets = ray_cells[batch_index] - anchor
        inside = (offsets >= 0) & (offsets < cell_count)
        clipped = jnp.clip(offsets, 0, cell_count - 1)
        picked = jnp.take(columns, clipped.reshape(-1), axis=1)
        picked = picked.reshape(columns.shape[0], clipped.shape[0], clipped.shape[1])
        weights_here = jnp.where(inside, ray_weights[batch_index], 0.0)
        partial_ens = jnp.einsum("mjk,jk->mj", picked, weights_here, precision=HIGHEST_PREC)
        prior_ens = sum_everywhere(partial_ens)
        increments, regress = innovations(prior_ens, obs_values[batch_index], obs_var[batch_index])
        columns = increment_block(columns, positions, increments, regress, ray_centers[batch_index], cell_count)
    return lax.all_to_all(columns, "mem", split_axis=0, concat_axis=1, tiled=True)


def lanes_of(shape):
    return lax.broadcasted_iota(jnp.int32, shape, 1)


def squeeze_rows(packed, weight, mask):
    rows = packed.shape[0]
    lane = lanes_of(packed.shape)
    marks = mask.astype(BF16)
    upper = lax.broadcasted_iota(jnp.int32, (LANES, LANES), 0) < lanes_of((LANES, LANES))
    before = jnp.dot(marks, upper.astype(BF16), preferred_element_type=F32)
    count = jnp.dot(marks, jnp.ones((LANES, LANES), BF16), preferred_element_type=F32).astype(jnp.int32)
    gap = jnp.where(mask, lane - before.astype(jnp.int32), -1)
    for bit in range(7):
        step = 1 << bit
        moved_gap = pltpu.roll(gap, LANES - step, 1)
        take = (moved_gap >= 0) & ((moved_gap & step) != 0)
        keep = (gap >= 0) & ((gap & step) == 0)
        packed = jnp.where(take, pltpu.roll(packed, LANES - step, 1), packed)
        weight = jnp.where(take, pltpu.roll(weight, LANES - step, 1), weight)
        gap = jnp.where(take, moved_gap, jnp.where(keep, gap, -1))
    while rows > 8:
        rows //= 2
        first, second = count[:rows], count[rows:]
        p2, w2 = packed[rows:], weight[rows:]
        for bit in range(7):
            step = 1 << bit
            far = (first & step) != 0
            p2 = jnp.where(far, pltpu.roll(p2, step, 1), p2)
            w2 = jnp.where(far, pltpu.roll(w2, step, 1), w2)
        own = lanes_of(first.shape) < first
        packed = jnp.where(own, packed[:rows], p2)
        weight = jnp.where(own, weight[:rows], w2)
        count = first + second
    return packed, weight, count


def pick_kernel(n_var, cells_in, weights_in, ens_ref, g_ref,
                cells_ref, weights_ref, ens_v, xt, graw, id_v, place_v, from_v, w_v, n_v, list_s, n_s, ens_sem, list_sem):
    members, span = ens_ref.shape
    nobs, kcells = cells_ref.shape[1:]
    rays_here = nobs // n_var
    load = pltpu.make_async_copy(ens_ref, ens_v, ens_sem)
    load.start()
    for batch in range(NBATCH):
        cells_ref[batch] = cells_in[batch].T
        weights_ref[batch] = weights_in[batch].T
    base = lax.axis_index("var") * span
    fold = LANES // kcells
    steps = rays_here // fold
    for part in range(n_var // 8):
        packs, weights = [], []
        for batch in range(NBATCH):
            for step in range(steps):
                rows = [pl.ds(part * 8 * rays_here + step + side * steps, 8, stride=rays_here) for side in range(fold)]
                place = jnp.concatenate([cells_ref[batch, row, :] for row in rows], axis=1) - base
                inside = (place >= 0) & (place < span)
                ray = batch * rays_here + step + lanes_of(place.shape) // kcells * steps
                packs.append(jnp.where(inside, jnp.bitwise_or(ray << 16, place & 0xFFFF), -1))
                weights.append(jnp.concatenate([weights_ref[batch, row, :] for row in rows], axis=1))
        packed = jnp.concatenate(packs, axis=0)
        packed, weight, count = squeeze_rows(packed, jnp.concatenate(weights, axis=0), packed >= 0)
        valid = lanes_of(count.shape) < count
        out_rows = pl.ds(part * 8, 8)
        place = jnp.where(valid, packed & 0xFFFF, 0)
        place_v[out_rows, :] = place
        from_v[out_rows, :] = ((place >> 9) << 7) | (place & 127)
        id_v[out_rows, :] = jnp.where(valid, packed >> 16, -1)
        w_v[out_rows, :] = jnp.where(valid, weight, 0.0)
        n_v[out_rows, :] = count
    to_list = pltpu.make_async_copy(from_v, list_s, list_sem.at[0])
    to_count = pltpu.make_async_copy(n_v, n_s, list_sem.at[1])
    to_list.start()
    to_count.start()
    load.wait()
    blank = jnp.zeros((32 - members, LANES), F32)

    def turn(step, carry):
        for group in range(4):
            tiles = []
            for part in range(4):
                at = pl.ds(pl.multiple_of(((step * 4 + group) * 4 + part) * LANES, LANES), LANES)
                tiles += [ens_v[:, at], blank]
            to = pl.ds(pl.multiple_of((step * 4 + group) * LANES, LANES), LANES)
            xt[to, :] = jnp.concatenate(tiles, axis=0).T
        return carry

    lax.fori_loop(0, span // (16 * LANES), turn, 0)
    to_list.wait()
    to_count.wait()

    def gather_row(row, carry):
        def gather_some(block, inner):
            found = []
            for unit in range(16):
                found.append(xt[pl.ds(list_s[row, block * 16 + unit], 1), :])
            for unit in range(16):
                graw[pl.ds(row * LANES + block * 16 + unit, 1), :] = found[unit]
            return inner

        lax.fori_loop(0, (jnp.minimum(n_s[row, 0], LANES) + 15) // 16, gather_some, 0)
        return carry

    lax.fori_loop(0, n_var, gather_row, 0)
    sub = lax.broadcasted_iota(jnp.int32, (24, LANES), 0)
    for row in range(n_var):
        raw = graw[pl.ds(row * LANES, LANES), :].T
        place = place_v[pl.ds(row, 1), :]
        ids = id_v[pl.ds(row, 1), :]
        quarter = (place >> 7) & 3
        total = jnp.zeros((24, LANES), F32)
        for piece in range(4):
            total = jnp.where(quarter == piece, raw[32 * piece:32 * piece + 24, :], total)
        total = jnp.where(ids >= 0, total, 0.0) * w_v[pl.ds(row, 1), :]
        total = jnp.where(sub == members, ids.astype(F32), total)
        g_ref[row] = jnp.where(sub == members + 1, place.astype(F32), total)


def pick(ensemble, ray_cells, ray_weights, n_var):
    members, span = ensemble.shape
    vmem = pl.BlockSpec(memory_space=pltpu.VMEM)
    return pl.pallas_call(
        functools.partial(pick_kernel, n_var),
        out_shape=jax.ShapeDtypeStruct((n_var, 24, LANES), F32),
        in_specs=[vmem, vmem, pl.BlockSpec(memory_space=pl.ANY)],
        out_specs=vmem,
        scratch_shapes=[
            pltpu.VMEM(ray_cells.shape, jnp.int32),
            pltpu.VMEM(ray_cells.shape, F32),
            pltpu.VMEM((members, span), F32),
            pltpu.VMEM((span // 4, LANES), F32),
            pltpu.VMEM((n_var * LANES, LANES), F32),
            pltpu.VMEM((n_var, LANES), jnp.int32),
            pltpu.VMEM((n_var, LANES), jnp.int32),
            pltpu.VMEM((n_var, LANES), jnp.int32),
            pltpu.VMEM((n_var, LANES), F32),
            pltpu.VMEM((n_var, LANES), jnp.int32),
            pltpu.SMEM((n_var, LANES), jnp.int32),
            pltpu.SMEM((n_var, LANES), jnp.int32),
            pltpu.SemaphoreType.DMA,
            pltpu.SemaphoreType.DMA((2,)),
        ],
        compiler_params=pltpu.CompilerParams(vmem_limit_bytes=48 << 20),
        cost_estimate=pl.CostEstimate(flops=1 << 30, bytes_accessed=64 << 20, transcendentals=0),
        name="pick",
    )(ray_cells.transpose(0, 2, 1), ray_weights.transpose(0, 2, 1), ensemble)


def high_dot(a, b):
    return jnp.dot(a, b, precision=HIGHEST_PREC, preferred_element_type=F32)


def split(x):
    high = x.astype(BF16)
    return high, (x - high.astype(F32)).astype(BF16)


def split_dot(a, b):
    a_high, a_low = split(a)
    b_high, b_low = split(b)
    total = jnp.dot(a_high, b_low, preferred_element_type=F32)
    total = total + jnp.dot(a_low, b_high, preferred_element_type=F32)
    return total + jnp.dot(a_high, b_high, preferred_element_type=F32)


def main_kernel(dims, ens_ref, g_ref, centers_ref, obs_ref, var_ref, early_refs, out_ref,
                par_ref, xf, res, xr, state, xb, agb, inc_v, reg_v, dpoly, dhi, dlo,
                mini_s, mini_r, fwd_s, fwd_r, own_sem, red_s, red_r, back_s, back_r):
    n_var, n_mem, members, cells, nobs, n_chunk = dims
    group = members // n_mem
    wide = 24 * n_mem
    sources = n_var // n_mem
    width = cells // n_chunk
    rays_here = nobs // n_var
    p, q = lax.axis_index("var"), lax.axis_index("mem")
    first = lax.rem(q + n_mem - p // sources, n_mem) * sources
    stays = p // sources == first // sources

    def var_peer(k):
        return {"var": lax.rem(p + k, n_var)}

    def mem_peer(k):
        return {"mem": lax.rem(q + k, n_mem)}

    barrier = pltpu.get_barrier_semaphore()

    def greet(k, carry):
        pl.semaphore_signal(barrier, inc=1, device_id=var_peer(k), device_id_type=MESH)
        return carry

    def greet_sender(k, carry):
        source, part = first + k // n_mem, lax.rem(k, n_mem)

        @pl.when((source != p) | (part != q))
        def _():
            pl.semaphore_signal(barrier, inc=1, device_id={"var": source, "mem": part}, device_id_type=MESH)

        return carry

    lax.fori_loop(0, n_var, greet_sender, 0)
    for k in range(1, n_mem):
        pl.semaphore_signal(barrier, inc=1, device_id=mem_peer(k), device_id_type=MESH)
    lax.fori_loop(1, n_var, greet, 0)
    lane = lanes_of((1, LANES))
    real_lane = (lax.rem(lane, 24) < group) & (lane < wide)
    block = p * n_mem + q
    rows = [centers_ref[...].astype(F32), obs_ref[...], var_ref[...]]
    rows.append(jnp.zeros((LANES - 3 * NBATCH, nobs), F32))
    par_ref[...] = jnp.concatenate(rows, axis=0).T
    pl.semaphore_wait(barrier, n_var - 1 + n_mem - 1 + n_var - stays.astype(jnp.int32))

    def send_mini(k, carry):
        there = lax.rem(p + k, n_var)
        taker = lax.rem(p // sources + there // sources, n_mem)

        @pl.when((k > 0) | jnp.logical_not(stays))
        def _():
            pltpu.make_async_remote_copy(
                src_ref=g_ref.at[there], dst_ref=xr.at[q, lax.rem(p, sources)],
                send_sem=mini_s, recv_sem=mini_r,
                device_id={"var": there, "mem": taker}, device_id_type=MESH).start()

        return carry

    lax.fori_loop(0, n_var, send_mini, 0)

    @pl.when(stays)
    def _():
        xr[q, lax.rem(p, sources)] = g_ref[p]

    def forward(k, chunk):
        there = lax.rem(q + k, n_mem)
        return pltpu.make_async_remote_copy(
            src_ref=ens_ref.at[:, pl.ds(pl.multiple_of(there * cells + chunk * width, LANES), width)],
            dst_ref=xf.at[q, :, pl.ds(pl.multiple_of(chunk * width, LANES), width)],
            send_sem=fwd_s.at[k, chunk], recv_sem=fwd_r.at[k, chunk],
            device_id=mem_peer(k), device_id_type=MESH)

    def start_forward(chunk, carry):
        for k in (2, 1, 3):
            forward(k, chunk).start()
        return carry

    paced = [EARLY]

    def pace(count):
        until = min(paced[0] + count, n_chunk)
        lax.fori_loop(paced[0], until, start_forward, 0)
        paced[0] = until

    pace(PACE[0])
    own = pltpu.make_async_copy(ens_ref.at[:, pl.ds(pl.multiple_of(q * cells, LANES), cells)], xf.at[q], own_sem.at[0])
    own.start()
    landing = []
    for k in range(1, n_mem):
        there = xf.at[lax.rem(q + n_mem - k, n_mem), :, pl.ds(0, EARLY * width)]
        landing.append(pltpu.make_async_copy(early_refs[k - 1], there, own_sem.at[1 + k]))
        landing[-1].start()

    def wait_mini(count):
        landed = g_ref.at[pl.ds(0, count)]
        pltpu.make_async_remote_copy(
            src_ref=landed, dst_ref=landed, send_sem=mini_s, recv_sem=mini_r,
            device_id=mem_peer(1), device_id_type=MESH).wait()

    @pl.when(stays)
    def _():
        wait_mini(n_var - 1)

    @pl.when(jnp.logical_not(stays))
    def _():
        wait_mini(n_var)

    sub = lax.broadcasted_iota(jnp.int32, (24, LANES), 0)
    ids, places = [], []
    for source in range(sources):
        for part in range(n_mem):
            tile = xr[part, source]
            state[pl.ds(part * 24, 24), pl.ds(source * LANES, LANES)] = jnp.where(sub < group, tile, 0.0)
        ids.append(xr[0, source, group:group + 1, :])
        places.append(xr[0, source, group + 1:group + 2, :] + ((first + source) * (n_mem * cells)).astype(F32))
    id_row = jnp.concatenate(ids, axis=1)
    scale = 1.0 / (LRAD * cells)
    place_row = jnp.concatenate(places, axis=1) * scale
    own_ray = lax.broadcasted_iota(jnp.int32, (rays_here, 1), 0).astype(F32)

    def own_rows():
        return pl.ds(pl.multiple_of(p * rays_here, rays_here), rays_here)

    def across(batch, k):
        return pltpu.make_async_remote_copy(
            src_ref=xb.at[batch, q], dst_ref=xb.at[batch, q],
            send_sem=red_s.at[batch, k], recv_sem=red_r.at[batch, k],
            device_id=mem_peer(k), device_id_type=MESH)

    def start_reduce(batch):
        chosen = (id_row == own_ray + batch * rays_here).astype(BF16)
        held = state[...]
        high = held.astype(BF16)
        rest = held - high.astype(F32)
        middle = rest.astype(BF16)
        low = (rest - middle.astype(F32)).astype(BF16)
        total = jnp.zeros((rays_here, wide), F32)
        for piece in (low, middle, high):
            total = total + lax.dot_general(chosen, piece, (((1,), (1,)), ((), ())), preferred_element_type=F32)
        xb[batch, q] = jnp.concatenate([total, jnp.zeros((rays_here, LANES - wide), F32)], axis=1)
        for k in (2, 1, 3):
            across(batch, k).start()

    def finish_reduce(batch):
        for k in (2, 1, 3):
            across(batch, k).wait()
        agb[batch, own_rows(), :] = jnp.sum(xb[batch], axis=0)
        mine = agb.at[batch, own_rows()]

        def send(k, carry):
            pltpu.make_async_remote_copy(
                src_ref=mine, dst_ref=mine,
                send_sem=red_s.at[batch, n_mem], recv_sem=red_r.at[batch, n_mem],
                device_id=var_peer(k), device_id_type=MESH).start()
            return carry

        lax.fori_loop(1, n_var, send, 0)
        pace(PACE[2])
        landed = agb.at[batch, pl.ds(0, nobs - rays_here)]
        pltpu.make_async_remote_copy(
            src_ref=landed, dst_ref=landed, send_sem=red_s.at[batch, n_mem], recv_sem=red_r.at[batch, n_mem],
            device_id=var_peer(1), device_id_type=MESH).wait()

    def innovate(batch):
        prior = agb[batch]
        obs = par_ref[:, NBATCH + batch:NBATCH + batch + 1]
        error_var = par_ref[:, 2 * NBATCH + batch:2 * NBATCH + batch + 1]
        mean = jnp.sum(prior, axis=1, keepdims=True) / members
        anomaly = jnp.where(real_lane, prior - mean, 0.0)
        variance = jnp.sum(anomaly * anomaly, axis=1, keepdims=True) / (members - 1) + EPSILON
        total_var = variance + error_var
        post_mean = (mean * error_var + obs * variance) / total_var
        shrink = jnp.sqrt(error_var / total_var)
        increments = jnp.where(real_lane, post_mean - mean + (shrink - 1.0) * anomaly, 0.0)
        inc_v[...] = increments.T
        reg_v[...] = anomaly / ((members - 1) * variance)

    def taper_at(batch, scaled):
        return 1.0 - jnp.abs(scaled - (par_ref[:, batch:batch + 1] + 0.5) * (cells * scale))

    def update_state(batch):
        slopes = split_dot(reg_v[:, 0:wide], state[...])
        slopes = slopes * jnp.maximum(taper_at(batch, place_row), 0.0)
        state[...] += split_dot(inc_v[0:wide, :], slopes)

    def compose(batch):
        for half in range(2):
            start = (block * cells + half * (cells // 2)).astype(F32) * scale
            near, far = taper_at(batch, start), taper_at(batch, start + (cells // 2) * scale)
            inside = near + far > 0.0
            alpha = jnp.where(inside, near, 0.0)
            beta = jnp.where(inside, far - near, 0.0)
            regress = reg_v[...]
            both = jnp.concatenate([regress * alpha, regress * beta], axis=1)
            ab = high_dot(inc_v[0:wide, :], both)
            a, b = ab[:, :LANES], ab[:, LANES:]
            if batch == 0:
                dpoly[half, 0], dpoly[half, 1] = a, b
                continue
            old = jnp.concatenate([dpoly[half, k] for k in range(batch + 1)], axis=1)
            left = jnp.concatenate([a[:, 0:wide], b[:, 0:wide]], axis=0)
            made = high_dot(left, old)
            for k in range(batch + 2):
                total = a if k == 0 else b if k == 1 else jnp.zeros_like(a)
                if k <= batch:
                    total = total + dpoly[half, k] + made[:wide, k * LANES:(k + 1) * LANES]
                if k >= 1:
                    total = total + made[wide:, (k - 1) * LANES:k * LANES]
                dpoly[half, k] = total

    start_reduce(0)
    for batch in range(NBATCH):
        pace(PACE[1])
        if batch:
            compose(batch - 1)
        finish_reduce(batch)
        pace(PACE[3])
        innovate(batch)
        if batch + 1 < NBATCH:
            update_state(batch)
            start_reduce(batch + 1)
    pace(n_chunk)
    compose(NBATCH - 1)

    terms = NBATCH + 1
    for half in range(2):
        for k in range(terms):
            high, low = split(dpoly[half, k][:, 0:wide])
            dhi[half, pl.ds(k * wide, wide), :] = high
            dlo[half, pl.ds(k * wide, wide), :] = low

    own.wait()
    for copy in landing:
        copy.wait()

    def back(k, chunk):
        there = lax.rem(q + k, n_mem)
        return pltpu.make_async_remote_copy(
            src_ref=res.at[there, :, pl.ds(pl.multiple_of(chunk * width, LANES), width)],
            dst_ref=out_ref.at[:, pl.ds(pl.multiple_of(q * cells + chunk * width, LANES), width)],
            send_sem=back_s.at[k], recv_sem=back_r.at[k],
            device_id=mem_peer(k), device_id_type=MESH)

    pad = jnp.zeros((24 - group, width), F32)

    def apply(chunk, carry):
        @pl.when(chunk >= EARLY)
        def _():
            for k in (2, 1, 3):
                forward(k, chunk).wait()

        half = chunk // (n_chunk // 2)
        at = pl.ds(pl.multiple_of(chunk * width, LANES), width)
        pieces = []
        for i in range(n_mem):
            pieces += [xf[i, :, at], pad]
        x = jnp.concatenate(pieces, axis=0)
        high, low = split(x)
        big, small = dhi[half], dlo[half]
        y = jnp.dot(big, high, preferred_element_type=F32)
        y = y + jnp.dot(big, low, preferred_element_type=F32)
        y = y + jnp.dot(small, high, preferred_element_type=F32)
        t = (lanes_of((1, width)) + (chunk - half * (n_chunk // 2)) * width).astype(F32) * (2.0 / cells)
        total = y[(terms - 1) * wide:]
        for k in range(terms - 2, -1, -1):
            total = y[k * wide:(k + 1) * wide] + t * total
        total = x + total
        for i in range(n_mem):
            res[i, :, at] = total[24 * i:24 * i + group]
        for k in (2, 1, 3):
            back(k, chunk).start()
        home = pl.ds(pl.multiple_of(q * cells + chunk * width, LANES), width)
        pltpu.make_async_copy(res.at[q, :, at], out_ref.at[:, home], own_sem.at[1]).start()
        return carry

    lax.fori_loop(0, n_chunk, apply, 0)
    mine = pl.ds(pl.multiple_of(q * cells, LANES), cells)
    keep = pltpu.make_async_copy(res.at[q], out_ref.at[:, mine], own_sem.at[1])
    for k in range(1, n_mem):
        source = lax.rem(q + n_mem - k, n_mem)
        landed = out_ref.at[:, pl.ds(pl.multiple_of(source * cells, LANES), cells)]
        pltpu.make_async_remote_copy(
            src_ref=res.at[lax.rem(q + k, n_mem)], dst_ref=landed, send_sem=back_s.at[k], recv_sem=back_r.at[k],
            device_id=mem_peer(k), device_id_type=MESH).wait()
    keep.wait()


def assimilate(ensemble, picked, ray_centers, obs_values, obs_var, early, n_var, n_mem):
    group, span = ensemble.shape
    cells = span // n_mem
    nobs = ray_centers.shape[1]
    wide = 24 * n_mem
    slots = n_var // n_mem * LANES
    rays_here = nobs // n_var
    vmem = pl.BlockSpec(memory_space=pltpu.VMEM)
    anywhere = pl.BlockSpec(memory_space=pl.ANY)
    dma = pltpu.SemaphoreType.DMA
    dims = (n_var, n_mem, group * n_mem, cells, nobs, N_CHUNK)
    return pl.pallas_call(
        functools.partial(main_kernel, dims),
        out_shape=jax.ShapeDtypeStruct((group, span), F32),
        in_specs=[anywhere, vmem, vmem, vmem, vmem, [anywhere] * len(early)],
        out_specs=anywhere,
        scratch_shapes=[
            pltpu.VMEM((nobs, LANES), F32),
            pltpu.VMEM((n_mem, group, cells), F32),
            pltpu.VMEM((n_mem, group, cells), F32),
            pltpu.VMEM((n_mem, n_var // n_mem, 24, LANES), F32),
            pltpu.VMEM((wide, slots), F32),
            pltpu.VMEM((NBATCH, n_mem, rays_here, LANES), F32),
            pltpu.VMEM((NBATCH, nobs, LANES), F32),
            pltpu.VMEM((LANES, nobs), F32),
            pltpu.VMEM((nobs, LANES), F32),
            pltpu.VMEM((2, NBATCH + 1, wide, LANES), F32),
            pltpu.VMEM((2, (NBATCH + 1) * wide, wide), BF16),
            pltpu.VMEM((2, (NBATCH + 1) * wide, wide), BF16),
            dma, dma,
            dma((n_mem, N_CHUNK)), dma((n_mem, N_CHUNK)),
            dma((1 + n_mem,)),
            dma((NBATCH, n_mem + 1)), dma((NBATCH, n_mem + 1)),
            dma((n_mem,)), dma((n_mem,)),
        ],
        compiler_params=pltpu.CompilerParams(collective_id=1, has_side_effects=True, vmem_limit_bytes=48 << 20),
        name="assimilate",
    )(ensemble, picked, ray_centers, obs_values, obs_var, early)


def first_columns(ensemble, n_mem):
    group, span = ensemble.shape
    cells = span // n_mem
    q = lax.axis_index("mem")
    arrived = []
    for k in range(1, n_mem):
        start = lax.rem(q + k, n_mem) * cells
        piece = lax.dynamic_slice(ensemble, (0, start), (group, EARLY * (cells // N_CHUNK)))
        arrived.append(lax.ppermute(piece, "mem", [(i, (i + k) % n_mem) for i in range(n_mem)]))
    return arrived


def fast(ensemble, ray_cells, ray_weights, ray_centers, obs_values, obs_var):
    n_var, n_mem = lax.axis_size("var"), lax.axis_size("mem")
    early = first_columns(ensemble, n_mem)
    picked = pick(ensemble, ray_cells, ray_weights, n_var)
    return assimilate(ensemble, picked, ray_centers, obs_values, obs_var, early, n_var, n_mem)


def fits(ray_cells, span, n_var):
    home = ray_cells.transpose(0, 2, 1) // span
    hits = home[:, :, None, :] == jnp.arange(n_var, dtype=jnp.int32)[:, None]
    by_ray = jnp.sum(hits.astype(jnp.int32), axis=(0, 1))
    return jnp.max(jnp.sum(by_ray.reshape(n_var, n_var, -1), axis=2)) <= LANES


def shards(*arrays):
    room = fits(arrays[1], arrays[0].shape[1], lax.axis_size("var"))
    return lax.cond(room, lambda made, *rest: made, lambda made, *rest: plain(*rest), fast(*arrays), *arrays)


def solution(mesh):
    placed = (P("mem", "var"), P(), P(), P(), P(), P())
    return jax.shard_map(
        shards, mesh=mesh, in_specs=placed, out_specs=P("mem", "var"), check_vma=False
    )
```

```python
import functools

import jax
import jax.numpy as jnp
from jax import lax
from jax.experimental import pallas as pl
from jax.experimental.pallas import tpu as pltpu
from jax.sharding import PartitionSpec as P

CELLS = 16384
NBATCH = 4
LRAD = 4
EPSILON = 1e-06
LANES = 128
HIGHEST_PREC = lax.Precision.HIGHEST
MESH = pl.DeviceIdType.MESH
N_CHUNK = 16
TAIL_PARTS = 4
FULL = 16
LAG = 3
EARLY = 6
PACE = (3, 1, 2, 0)
BF16 = jnp.bfloat16
F32 = jnp.float32


def innovations(prior_ens, obs_now, error_var):
    members = prior_ens.shape[0]
    prior_mean = jnp.mean(prior_ens, axis=0)
    anomaly = prior_ens - prior_mean
    variance = jnp.sum(anomaly * anomaly, axis=0) / (members - 1) + EPSILON
    total_var = variance + error_var
    post_mean = (prior_mean * error_var + obs_now * variance) / total_var
    shrink = jnp.sqrt(error_var / total_var)
    increments = post_mean - prior_mean + (shrink - 1.0) * anomaly
    regress = anomaly / ((members - 1) * variance)
    return (increments, regress)


def taper_weights(positions, centers, cells):
    centre_pos = (centers.astype(jnp.float32) + 0.5) * cells
    distance = jnp.abs(positions[None, :] - centre_pos[:, None]) / (LRAD * cells)
    return jnp.maximum(0.0, 1.0 - distance)


def increment_block(cell_block, positions, increments, regress, centers, cells):
    slopes = jnp.dot(regress.T, cell_block, precision=HIGHEST_PREC)
    slopes = slopes * taper_weights(positions, centers, cells)
    return cell_block + jnp.dot(increments, slopes, precision=HIGHEST_PREC)


def sum_everywhere(partial_ens):
    axes = ("var", "mem")
    count = lax.axis_size("var") * lax.axis_size("mem")
    members, rays = partial_ens.shape
    pieces = partial_ens.reshape(members, count, rays // count).transpose(1, 0, 2)
    total = jnp.sum(lax.all_to_all(pieces, axes, split_axis=0, concat_axis=0, tiled=True), axis=0)
    copies = jnp.broadcast_to(total, pieces.shape)
    whole = lax.all_to_all(copies, axes, split_axis=0, concat_axis=0, tiled=True)
    return whole.transpose(1, 0, 2).reshape(members, rays)


def plain(ensemble, ray_cells, ray_weights, ray_centers, obs_values, obs_var):
    groups = lax.axis_size("mem")
    cell_count = ensemble.shape[1] // groups
    anchor = (lax.axis_index("var") * groups + lax.axis_index("mem")) * cell_count
    positions = (anchor + jnp.arange(cell_count, dtype=jnp.int32)).astype(jnp.float32)
    columns = lax.all_to_all(ensemble, "mem", split_axis=1, concat_axis=0, tiled=True)
    for batch_index in range(NBATCH):
        offsets = ray_cells[batch_index] - anchor
        inside = (offsets >= 0) & (offsets < cell_count)
        clipped = jnp.clip(offsets, 0, cell_count - 1)
        picked = jnp.take(columns, clipped.reshape(-1), axis=1)
        picked = picked.reshape(columns.shape[0], clipped.shape[0], clipped.shape[1])
        weights_here = jnp.where(inside, ray_weights[batch_index], 0.0)
        partial_ens = jnp.einsum("mjk,jk->mj", picked, weights_here, precision=HIGHEST_PREC)
        prior_ens = sum_everywhere(partial_ens)
        increments, regress = innovations(prior_ens, obs_values[batch_index], obs_var[batch_index])
        columns = increment_block(columns, positions, increments, regress, ray_centers[batch_index], cell_count)
    return lax.all_to_all(columns, "mem", split_axis=0, concat_axis=1, tiled=True)


def lanes_of(shape):
    return lax.broadcasted_iota(jnp.int32, shape, 1)


def squeeze_rows(packed, weight, mask):
    rows = packed.shape[0]
    lane = lanes_of(packed.shape)
    marks = mask.astype(BF16)
    upper = lax.broadcasted_iota(jnp.int32, (LANES, LANES), 0) < lanes_of((LANES, LANES))
    before = jnp.dot(marks, upper.astype(BF16), preferred_element_type=F32)
    count = jnp.dot(marks, jnp.ones((LANES, LANES), BF16), preferred_element_type=F32).astype(jnp.int32)
    gap = jnp.where(mask, lane - before.astype(jnp.int32), -1)
    for bit in range(7):
        step = 1 << bit
        moved_gap = pltpu.roll(gap, LANES - step, 1)
        take = (moved_gap >= 0) & ((moved_gap & step) != 0)
        keep = (gap >= 0) & ((gap & step) == 0)
        packed = jnp.where(take, pltpu.roll(packed, LANES - step, 1), packed)
        weight = jnp.where(take, pltpu.roll(weight, LANES - step, 1), weight)
        gap = jnp.where(take, moved_gap, jnp.where(keep, gap, -1))
    while rows > 8:
        rows //= 2
        first, second = count[:rows], count[rows:]
        p2, w2 = packed[rows:], weight[rows:]
        for bit in range(7):
            step = 1 << bit
            far = (first & step) != 0
            p2 = jnp.where(far, pltpu.roll(p2, step, 1), p2)
            w2 = jnp.where(far, pltpu.roll(w2, step, 1), w2)
        own = lanes_of(first.shape) < first
        packed = jnp.where(own, packed[:rows], p2)
        weight = jnp.where(own, weight[:rows], w2)
        count = first + second
    return packed, weight, count


def pick_kernel(n_var, n_mem, cells_in, weights_in, ens_ref, g_ref, tails_ref,
                cells_ref, weights_ref, ens_v, xt, graw, id_v, place_v, from_v, w_v, n_v, list_s, n_s, ens_sem, list_sem):
    members, span = ens_ref.shape
    nobs, kcells = cells_ref.shape[1:]
    rays_here = nobs // n_var
    load = pltpu.make_async_copy(ens_ref, ens_v, ens_sem)
    load.start()
    for batch in range(NBATCH):
        cells_ref[batch] = cells_in[batch].T
        weights_ref[batch] = weights_in[batch].T
    base = lax.axis_index("var") * span
    fold = LANES // kcells
    steps = rays_here // fold
    for part in range(n_var // 8):
        packs, weights = [], []
        for batch in range(NBATCH):
            for step in range(steps):
                rows = [pl.ds(part * 8 * rays_here + step + side * steps, 8, stride=rays_here) for side in range(fold)]
                place = jnp.concatenate([cells_ref[batch, row, :] for row in rows], axis=1) - base
                inside = (place >= 0) & (place < span)
                ray = batch * rays_here + step + lanes_of(place.shape) // kcells * steps
                packs.append(jnp.where(inside, jnp.bitwise_or(ray << 16, place & 0xFFFF), -1))
                weights.append(jnp.concatenate([weights_ref[batch, row, :] for row in rows], axis=1))
        packed = jnp.concatenate(packs, axis=0)
        packed, weight, count = squeeze_rows(packed, jnp.concatenate(weights, axis=0), packed >= 0)
        valid = lanes_of(count.shape) < count
        out_rows = pl.ds(part * 8, 8)
        place = jnp.where(valid, packed & 0xFFFF, 0)
        place_v[out_rows, :] = place
        from_v[out_rows, :] = ((place >> 9) << 7) | (place & 127)
        id_v[out_rows, :] = jnp.where(valid, packed >> 16, -1)
        w_v[out_rows, :] = jnp.where(valid, weight, 0.0)
        n_v[out_rows, :] = count
    to_list = pltpu.make_async_copy(from_v, list_s, list_sem.at[0])
    to_count = pltpu.make_async_copy(n_v, n_s, list_sem.at[1])
    to_list.start()
    to_count.start()
    load.wait()
    blank = jnp.zeros((32 - members, LANES), F32)
    half, step = span // n_mem // 2, 8 * LANES

    def fold_rows(index, carry):
        group, at = index // (half // step), lax.rem(index, half // step) * step
        ends = []
        for side in range(2):
            columns = pl.ds(pl.multiple_of((group * 2 + side) * half + at, LANES), step)
            ends.append(ens_v[FULL:, columns])
        tails_ref[group, :, pl.ds(pl.multiple_of(at, LANES), step)] = jnp.concatenate(ends, axis=0)
        return carry

    lax.fori_loop(0, n_mem * (half // step), fold_rows, 0)

    def turn(step, carry):
        for group in range(4):
            tiles = []
            for part in range(4):
                at = pl.ds(pl.multiple_of(((step * 4 + group) * 4 + part) * LANES, LANES), LANES)
                tiles += [ens_v[:, at], blank]
            to = pl.ds(pl.multiple_of((step * 4 + group) * LANES, LANES), LANES)
            xt[to, :] = jnp.concatenate(tiles, axis=0).T
        return carry

    lax.fori_loop(0, span // (16 * LANES), turn, 0)
    to_list.wait()
    to_count.wait()

    def gather_row(row, carry):
        def gather_some(block, inner):
            found = []
            for unit in range(16):
                found.append(xt[pl.ds(list_s[row, block * 16 + unit], 1), :])
            for unit in range(16):
                graw[pl.ds(row * LANES + block * 16 + unit, 1), :] = found[unit]
            return inner

        lax.fori_loop(0, (jnp.minimum(n_s[row, 0], LANES) + 15) // 16, gather_some, 0)
        return carry

    lax.fori_loop(0, n_var, gather_row, 0)
    sub = lax.broadcasted_iota(jnp.int32, (24, LANES), 0)
    for row in range(n_var):
        raw = graw[pl.ds(row * LANES, LANES), :].T
        place = place_v[pl.ds(row, 1), :]
        ids = id_v[pl.ds(row, 1), :]
        quarter = (place >> 7) & 3
        total = jnp.zeros((24, LANES), F32)
        for piece in range(4):
            total = jnp.where(quarter == piece, raw[32 * piece:32 * piece + 24, :], total)
        total = jnp.where(ids >= 0, total, 0.0) * w_v[pl.ds(row, 1), :]
        total = jnp.where(sub == members, ids.astype(F32), total)
        total = jnp.where(sub == members + 1, place.astype(F32), total)
        g_ref[row] = jnp.where(sub == members + 2, n_v[pl.ds(row, 1), :].astype(F32), total)


def pick(ensemble, ray_cells, ray_weights, n_var, n_mem):
    members, span = ensemble.shape
    vmem = pl.BlockSpec(memory_space=pltpu.VMEM)
    return pl.pallas_call(
        functools.partial(pick_kernel, n_var, n_mem),
        out_shape=(
            jax.ShapeDtypeStruct((n_var, 24, LANES), F32),
            jax.ShapeDtypeStruct((n_mem, 2 * (members - FULL), span // n_mem // 2), F32),
        ),
        in_specs=[vmem, vmem, pl.BlockSpec(memory_space=pl.ANY)],
        out_specs=(vmem, vmem),
        scratch_shapes=[
            pltpu.VMEM(ray_cells.shape, jnp.int32),
            pltpu.VMEM(ray_cells.shape, F32),
            pltpu.VMEM((members, span), F32),
            pltpu.VMEM((span // 4, LANES), F32),
            pltpu.VMEM((n_var * LANES, LANES), F32),
            pltpu.VMEM((n_var, LANES), jnp.int32),
            pltpu.VMEM((n_var, LANES), jnp.int32),
            pltpu.VMEM((n_var, LANES), jnp.int32),
            pltpu.VMEM((n_var, LANES), F32),
            pltpu.VMEM((n_var, LANES), jnp.int32),
            pltpu.SMEM((n_var, LANES), jnp.int32),
            pltpu.SMEM((n_var, LANES), jnp.int32),
            pltpu.SemaphoreType.DMA,
            pltpu.SemaphoreType.DMA((2,)),
        ],
        compiler_params=pltpu.CompilerParams(vmem_limit_bytes=48 << 20),
        cost_estimate=pl.CostEstimate(flops=1 << 30, bytes_accessed=64 << 20, transcendentals=0),
        name="pick",
    )(ray_cells.transpose(0, 2, 1), ray_weights.transpose(0, 2, 1), ensemble)


def high_dot(a, b):
    return jnp.dot(a, b, precision=HIGHEST_PREC, preferred_element_type=F32)


def split(x):
    high = x.astype(BF16)
    return high, (x - high.astype(F32)).astype(BF16)


def split_dot(a, b):
    a_high, a_low = split(a)
    b_high, b_low = split(b)
    total = jnp.dot(a_high, b_low, preferred_element_type=F32)
    total = total + jnp.dot(a_low, b_high, preferred_element_type=F32)
    return total + jnp.dot(a_high, b_high, preferred_element_type=F32)


def main_kernel(dims, ens_ref, tails_ref, g_ref, centers_ref, obs_ref, var_ref, early_refs, out_ref, full_ref,
                par_ref, xf, xtail, res, rtail, out_v, otail, xr, state, xb, agb, inc_v, reg_v, dpoly, dhi, dlo,
                mini_s, mini_r, fwd_s, fwd_r, tail_s, tail_r, own_sem, red_s, red_r, back_s, back_r, store_s):
    n_var, n_mem, members, cells, nobs, n_chunk = dims
    group = members // n_mem
    wide = 24 * n_mem
    sources = n_var // n_mem
    width = cells // n_chunk
    rays_here = nobs // n_var
    p, q = lax.axis_index("var"), lax.axis_index("mem")
    first = lax.rem(q + n_mem - p // sources, n_mem) * sources
    stays = p // sources == first // sources

    def var_peer(k):
        return {"var": lax.rem(p + k, n_var)}

    def mem_peer(k):
        return {"mem": lax.rem(q + k, n_mem)}

    barrier = pltpu.get_barrier_semaphore()

    def greet(k, carry):
        pl.semaphore_signal(barrier, inc=1, device_id=var_peer(k), device_id_type=MESH)
        return carry

    def greet_sender(k, carry):
        source, part = first + k // n_mem, lax.rem(k, n_mem)

        @pl.when((source != p) | (part != q))
        def _():
            pl.semaphore_signal(barrier, inc=1, device_id={"var": source, "mem": part}, device_id_type=MESH)

        return carry

    lax.fori_loop(0, n_var, greet_sender, 0)
    for k in range(1, n_mem):
        pl.semaphore_signal(barrier, inc=1, device_id=mem_peer(k), device_id_type=MESH)
    lax.fori_loop(1, n_var, greet, 0)
    lane = lanes_of((1, LANES))
    real_lane = (lax.rem(lane, 24) < group) & (lane < wide)
    block = p * n_mem + q
    rows = [centers_ref[...].astype(F32), obs_ref[...], var_ref[...]]
    rows.append(jnp.zeros((LANES - 3 * NBATCH, nobs), F32))
    par_ref[...] = jnp.concatenate(rows, axis=0).T
    pl.semaphore_wait(barrier, n_var - 1 + n_mem - 1 + n_var - stays.astype(jnp.int32))

    def send_mini(k, carry):
        there = lax.rem(p + k, n_var)
        taker = lax.rem(p // sources + there // sources, n_mem)

        @pl.when((k > 0) | jnp.logical_not(stays))
        def _():
            pltpu.make_async_remote_copy(
                src_ref=g_ref.at[there], dst_ref=xr.at[q, lax.rem(p, sources)],
                send_sem=mini_s, recv_sem=mini_r,
                device_id={"var": there, "mem": taker}, device_id_type=MESH).start()

        return carry

    lax.fori_loop(0, n_var, send_mini, 0)

    @pl.when(stays)
    def _():
        xr[q, lax.rem(p, sources)] = g_ref[p]

    def forward(k, chunk):
        there = lax.rem(q + k, n_mem)
        return pltpu.make_async_remote_copy(
            src_ref=ens_ref.at[pl.ds(0, FULL), pl.ds(pl.multiple_of(there * cells + chunk * width, LANES), width)],
            dst_ref=xf.at[q, :, pl.ds(pl.multiple_of(chunk * width, LANES), width)],
            send_sem=fwd_s.at[k, chunk], recv_sem=fwd_r.at[k, chunk],
            device_id=mem_peer(k), device_id_type=MESH)

    def start_forward(chunk, carry):
        for k in (2, 1, 3):
            forward(k, chunk).start()
        return carry

    def forward_tail(k, part):
        columns = pl.ds(part * (cells // 2 // TAIL_PARTS), cells // 2 // TAIL_PARTS)
        return pltpu.make_async_remote_copy(
            src_ref=tails_ref.at[lax.rem(q + k, n_mem), :, columns], dst_ref=xtail.at[q, :, columns],
            send_sem=tail_s.at[k, part], recv_sem=tail_r.at[k, part],
            device_id=mem_peer(k), device_id_type=MESH)

    paced = [EARLY - TAIL_PARTS]

    def pace(count):
        while count > 0 and paced[0] < EARLY:
            for k in (2, 1, 3):
                forward_tail(k, paced[0] - EARLY + TAIL_PARTS).start()
            paced[0] += 1
            count -= 1
        until = min(paced[0] + count, n_chunk)
        if until > paced[0]:
            lax.fori_loop(paced[0], until, start_forward, 0)
            paced[0] = until

    pace(PACE[0])
    mine = pl.ds(pl.multiple_of(q * cells, LANES), cells)
    landing = [
        pltpu.make_async_copy(ens_ref.at[pl.ds(0, FULL), mine], xf.at[q], own_sem.at[0]),
        pltpu.make_async_copy(tails_ref.at[q], xtail.at[q], own_sem.at[1]),
    ]
    for k in range(1, n_mem):
        there = xf.at[lax.rem(q + n_mem - k, n_mem), :, pl.ds(0, EARLY * width)]
        landing.append(pltpu.make_async_copy(early_refs[k - 1], there, own_sem.at[1 + k]))
    for copy in landing:
        copy.start()

    def wait_mini(count):
        landed = g_ref.at[pl.ds(0, count)]
        pltpu.make_async_remote_copy(
            src_ref=landed, dst_ref=landed, send_sem=mini_s, recv_sem=mini_r,
            device_id=mem_peer(1), device_id_type=MESH).wait()

    @pl.when(stays)
    def _():
        wait_mini(n_var - 1)

    @pl.when(jnp.logical_not(stays))
    def _():
        wait_mini(n_var)

    sub = lax.broadcasted_iota(jnp.int32, (24, LANES), 0)
    ids, places = [], []
    most = jnp.zeros((1, LANES), F32)
    for source in range(sources):
        for part in range(n_mem):
            tile = xr[part, source]
            state[pl.ds(part * 24, 24), pl.ds(source * LANES, LANES)] = jnp.where(sub < group, tile, 0.0)
        ids.append(xr[0, source, group:group + 1, :])
        most = jnp.maximum(most, xr[0, source, group + 2:group + 3, :])
        places.append(xr[0, source, group + 1:group + 2, :] + ((first + source) * (n_mem * cells)).astype(F32))
    id_row = jnp.concatenate(ids, axis=1)
    scale = 1.0 / (LRAD * cells)
    place_row = jnp.concatenate(places, axis=1) * scale
    own_ray = lax.broadcasted_iota(jnp.int32, (rays_here, 1), 0).astype(F32)

    def own_rows():
        return pl.ds(pl.multiple_of(p * rays_here, rays_here), rays_here)

    def across(batch, k):
        return pltpu.make_async_remote_copy(
            src_ref=xb.at[batch, q], dst_ref=xb.at[batch, q],
            send_sem=red_s.at[batch, k], recv_sem=red_r.at[batch, k],
            device_id=mem_peer(k), device_id_type=MESH)

    def start_reduce(batch):
        chosen = (id_row == own_ray + batch * rays_here).astype(BF16)
        held = state[...]
        high = held.astype(BF16)
        rest = held - high.astype(F32)
        middle = rest.astype(BF16)
        low = (rest - middle.astype(F32)).astype(BF16)
        total = jnp.zeros((rays_here, wide), F32)
        for piece in (low, middle, high):
            total = total + lax.dot_general(chosen, piece, (((1,), (1,)), ((), ())), preferred_element_type=F32)
        over = jnp.broadcast_to((most > LANES).astype(F32), (rays_here, LANES))
        xb[batch, q] = jnp.concatenate([total, over[:, wide:]], axis=1)
        for k in (2, 1, 3):
            across(batch, k).start()

    def finish_reduce(batch):
        for k in (2, 1, 3):
            across(batch, k).wait()
        agb[batch, own_rows(), :] = jnp.sum(xb[batch], axis=0)
        mine = agb.at[batch, own_rows()]

        def send(k, carry):
            pltpu.make_async_remote_copy(
                src_ref=mine, dst_ref=mine,
                send_sem=red_s.at[batch, n_mem], recv_sem=red_r.at[batch, n_mem],
                device_id=var_peer(k), device_id_type=MESH).start()
            return carry

        lax.fori_loop(1, n_var, send, 0)
        pace(PACE[2])
        landed = agb.at[batch, pl.ds(0, nobs - rays_here)]
        pltpu.make_async_remote_copy(
            src_ref=landed, dst_ref=landed, send_sem=red_s.at[batch, n_mem], recv_sem=red_r.at[batch, n_mem],
            device_id=var_peer(1), device_id_type=MESH).wait()

    def innovate(batch):
        prior = agb[batch]
        obs = par_ref[:, NBATCH + batch:NBATCH + batch + 1]
        error_var = par_ref[:, 2 * NBATCH + batch:2 * NBATCH + batch + 1]
        mean = jnp.sum(jnp.where(real_lane, prior, 0.0), axis=1, keepdims=True) / members
        anomaly = jnp.where(real_lane, prior - mean, 0.0)
        variance = jnp.sum(anomaly * anomaly, axis=1, keepdims=True) / (members - 1) + EPSILON
        total_var = variance + error_var
        post_mean = (mean * error_var + obs * variance) / total_var
        shrink = jnp.sqrt(error_var / total_var)
        increments = jnp.where(real_lane, post_mean - mean + (shrink - 1.0) * anomaly, 0.0)
        inc_v[...] = increments.T
        reg_v[...] = anomaly / ((members - 1) * variance)

    def taper_at(batch, scaled):
        return 1.0 - jnp.abs(scaled - (par_ref[:, batch:batch + 1] + 0.5) * (cells * scale))

    def update_state(batch):
        slopes = split_dot(reg_v[:, 0:wide], state[...])
        slopes = slopes * jnp.maximum(taper_at(batch, place_row), 0.0)
        state[...] += split_dot(inc_v[0:wide, :], slopes)

    def compose(batch):
        for half in range(2):
            start = (block * cells + half * (cells // 2)).astype(F32) * scale
            near, far = taper_at(batch, start), taper_at(batch, start + (cells // 2) * scale)
            inside = near + far > 0.0
            alpha = jnp.where(inside, near, 0.0)
            beta = jnp.where(inside, far - near, 0.0)
            regress = reg_v[...]
            both = jnp.concatenate([regress * alpha, regress * beta], axis=1)
            ab = high_dot(inc_v[0:wide, :], both)
            a, b = ab[:, :LANES], ab[:, LANES:]
            if batch == 0:
                dpoly[half, 0], dpoly[half, 1] = a, b
                continue
            old = jnp.concatenate([dpoly[half, k] for k in range(batch + 1)], axis=1)
            left = jnp.concatenate([a[:, 0:wide], b[:, 0:wide]], axis=0)
            made = high_dot(left, old)
            for k in range(batch + 2):
                total = a if k == 0 else b if k == 1 else jnp.zeros_like(a)
                if k <= batch:
                    total = total + dpoly[half, k] + made[:wide, k * LANES:(k + 1) * LANES]
                if k >= 1:
                    total = total + made[wide:, (k - 1) * LANES:k * LANES]
                dpoly[half, k] = total

    start_reduce(0)
    for batch in range(NBATCH):
        pace(PACE[1])
        if batch:
            compose(batch - 1)
        finish_reduce(batch)
        pace(PACE[3])
        innovate(batch)
        if batch + 1 < NBATCH:
            update_state(batch)
            start_reduce(batch + 1)
    pace(n_chunk)
    compose(NBATCH - 1)

    terms = NBATCH + 1
    for half in range(2):
        for k in range(terms):
            high, low = split(dpoly[half, k][:, 0:wide])
            dhi[half, pl.ds(k * wide, wide), :] = high
            dlo[half, pl.ds(k * wide, wide), :] = low

    full_ref[...] = jnp.max(agb[0], axis=0, keepdims=True)
    for copy in landing:
        copy.wait()
    for k in (2, 1, 3):
        for part in range(TAIL_PARTS):
            forward_tail(k, part).wait()

    pairs = n_chunk // 2
    rest = group - FULL

    def columns_of(block_index, pair, side):
        return pl.ds(pl.multiple_of(block_index * cells + (side * pairs + pair) * width, LANES), width)

    def back(k, pair):
        there = lax.rem(q + k, n_mem)
        tail = pl.ds(pl.multiple_of(pair * width, LANES), width)
        ends = [(res.at[there, :, columns_of(0, pair, side)], out_v.at[pl.ds(0, FULL), columns_of(q, pair, side)])
                for side in range(2)]
        ends.append((rtail.at[there, :, tail], otail.at[q, :, tail]))
        if k == 0:
            return [pltpu.make_async_copy(a, b, back_r.at[0, pair, n]) for n, (a, b) in enumerate(ends)]
        return [pltpu.make_async_remote_copy(
            src_ref=a, dst_ref=b, send_sem=back_s.at[k, pair, n], recv_sem=back_r.at[k, pair, n],
            device_id=mem_peer(k), device_id_type=MESH) for n, (a, b) in enumerate(ends)]

    def store(source, pair, side):
        columns = columns_of(source, pair, side)
        return pltpu.make_async_copy(out_v.at[:, columns], out_ref.at[:, columns], store_s.at[source])

    def drain(pair):
        tail = pl.ds(pl.multiple_of(pair * width, LANES), width)
        for k in (0, 1, 3, 2):
            source = lax.rem(q + n_mem - k, n_mem)
            for copy in back(k, pair):
                copy.wait()
            folded = otail[source, :, tail]
            for side in range(2):
                out_v[FULL:, columns_of(source, pair, side)] = folded[side * rest:(side + 1) * rest]
                store(source, pair, side).start()

    pad = jnp.zeros((24 - group, width), F32)

    def apply(pair, carry):
        tail = pl.ds(pl.multiple_of(pair * width, LANES), width)
        for side in range(2):
            chunk = side * pairs + pair

            @pl.when(chunk >= EARLY)
            def _():
                for k in (2, 1, 3):
                    forward(k, chunk).wait()

            at = pl.ds(pl.multiple_of(chunk * width, LANES), width)
            pieces = []
            for i in range(n_mem):
                pieces += [xf[i, :, at], xtail[i, side * rest:(side + 1) * rest, tail], pad]
            x = jnp.concatenate(pieces, axis=0)
            high, low = split(x)
            big, small = dhi[side], dlo[side]
            y = jnp.dot(big, high, preferred_element_type=F32)
            y = y + jnp.dot(big, low, preferred_element_type=F32)
            y = y + jnp.dot(small, high, preferred_element_type=F32)
            t = (lanes_of((1, width)) + pair * width).astype(F32) * (2.0 / cells)
            total = y[(terms - 1) * wide:]
            for k in range(terms - 2, -1, -1):
                total = y[k * wide:(k + 1) * wide] + t * total
            total = x + total
            for i in range(n_mem):
                res[i, :, at] = total[24 * i:24 * i + FULL]
                rtail[i, side * rest:(side + 1) * rest, tail] = total[24 * i + FULL:24 * i + group]
        for k in (2, 1, 3, 0):
            for copy in back(k, pair):
                copy.start()

        @pl.when(pair >= LAG)
        def _():
            drain(pair - LAG)

        return carry

    lax.fori_loop(0, pairs, apply, 0)

    def drain_rest(pair, carry):
        drain(pair)
        return carry

    lax.fori_loop(pairs - LAG, pairs, drain_rest, 0)
    for source in range(n_mem):
        columns = pl.ds(source * cells, cells)
        pltpu.make_async_copy(out_v.at[:, columns], out_ref.at[:, columns], store_s.at[source]).wait()


def assimilate(ensemble, tails, picked, ray_centers, obs_values, obs_var, early, n_var, n_mem):
    group, span = ensemble.shape
    cells = span // n_mem
    nobs = ray_centers.shape[1]
    wide = 24 * n_mem
    slots = n_var // n_mem * LANES
    rays_here = nobs // n_var
    vmem = pl.BlockSpec(memory_space=pltpu.VMEM)
    anywhere = pl.BlockSpec(memory_space=pl.ANY)
    dma = pltpu.SemaphoreType.DMA
    dims = (n_var, n_mem, group * n_mem, cells, nobs, N_CHUNK)
    return pl.pallas_call(
        functools.partial(main_kernel, dims),
        out_shape=(jax.ShapeDtypeStruct((group, span), F32), jax.ShapeDtypeStruct((1, LANES), F32)),
        in_specs=[anywhere, anywhere, vmem, vmem, vmem, vmem, [anywhere] * len(early)],
        out_specs=(anywhere, vmem),
        scratch_shapes=[
            pltpu.VMEM((nobs, LANES), F32),
            pltpu.VMEM((n_mem, FULL, cells), F32),
            pltpu.VMEM(tails.shape, F32),
            pltpu.VMEM((n_mem, FULL, cells), F32),
            pltpu.VMEM(tails.shape, F32),
            pltpu.VMEM((group, span), F32),
            pltpu.VMEM(tails.shape, F32),
            pltpu.VMEM((n_mem, n_var // n_mem, 24, LANES), F32),
            pltpu.VMEM((wide, slots), F32),
            pltpu.VMEM((NBATCH, n_mem, rays_here, LANES), F32),
            pltpu.VMEM((NBATCH, nobs, LANES), F32),
            pltpu.VMEM((LANES, nobs), F32),
            pltpu.VMEM((nobs, LANES), F32),
            pltpu.VMEM((2, NBATCH + 1, wide, LANES), F32),
            pltpu.VMEM((2, (NBATCH + 1) * wide, wide), BF16),
            pltpu.VMEM((2, (NBATCH + 1) * wide, wide), BF16),
            dma, dma,
            dma((n_mem, N_CHUNK)), dma((n_mem, N_CHUNK)),
            dma((n_mem, TAIL_PARTS)), dma((n_mem, TAIL_PARTS)),
            dma((1 + n_mem,)),
            dma((NBATCH, n_mem + 1)), dma((NBATCH, n_mem + 1)),
            dma((n_mem, N_CHUNK // 2, 3)), dma((n_mem, N_CHUNK // 2, 3)),
            dma((n_mem,)),
        ],
        compiler_params=pltpu.CompilerParams(collective_id=1, has_side_effects=True, vmem_limit_bytes=48 << 20),
        name="assimilate",
    )(ensemble, tails, picked, ray_centers, obs_values, obs_var, early)


def first_columns(ensemble, n_mem):
    group, span = ensemble.shape
    cells = span // n_mem
    q = lax.axis_index("mem")
    arrived = []
    for k in range(1, n_mem):
        start = lax.rem(q + k, n_mem) * cells
        piece = lax.dynamic_slice(ensemble, (0, start), (FULL, EARLY * (cells // N_CHUNK)))
        arrived.append(lax.ppermute(piece, "mem", [(i, (i + k) % n_mem) for i in range(n_mem)]))
    return arrived


def fast(ensemble, ray_cells, ray_weights, ray_centers, obs_values, obs_var):
    n_var, n_mem = lax.axis_size("var"), lax.axis_size("mem")
    early = first_columns(ensemble, n_mem)
    picked, tails = pick(ensemble, ray_cells, ray_weights, n_var, n_mem)
    return assimilate(ensemble, tails, picked, ray_centers, obs_values, obs_var, early, n_var, n_mem)


def shards(*arrays):
    made, full = fast(*arrays)
    return lax.cond(full[0, LANES - 1] < 0.5, lambda made, *rest: made, lambda made, *rest: plain(*rest), made, *arrays)


def solution(mesh):
    placed = (P("mem", "var"), P(), P(), P(), P(), P())
    return jax.shard_map(
        shards, mesh=mesh, in_specs=placed, out_specs=P("mem", "var"), check_vma=False
    )
```

```python
import functools

import jax
import jax.numpy as jnp
from jax import lax
from jax.experimental import pallas as pl
from jax.experimental.pallas import tpu as pltpu
from jax.sharding import PartitionSpec as P

CELLS = 16384
NBATCH = 4
LRAD = 4
EPSILON = 1e-06
LANES = 128
HIGHEST_PREC = lax.Precision.HIGHEST
MESH = pl.DeviceIdType.MESH
N_CHUNK = 16
TAIL_PARTS = 4
FULL = 16
LAG = 3
EARLY = 6
PACE = (3, 1, 2, 0)
BF16 = jnp.bfloat16
F32 = jnp.float32


def innovations(prior_ens, obs_now, error_var):
    members = prior_ens.shape[0]
    prior_mean = jnp.mean(prior_ens, axis=0)
    anomaly = prior_ens - prior_mean
    variance = jnp.sum(anomaly * anomaly, axis=0) / (members - 1) + EPSILON
    total_var = variance + error_var
    post_mean = (prior_mean * error_var + obs_now * variance) / total_var
    shrink = jnp.sqrt(error_var / total_var)
    increments = post_mean - prior_mean + (shrink - 1.0) * anomaly
    regress = anomaly / ((members - 1) * variance)
    return (increments, regress)


def taper_weights(positions, centers, cells):
    centre_pos = (centers.astype(jnp.float32) + 0.5) * cells
    distance = jnp.abs(positions[None, :] - centre_pos[:, None]) / (LRAD * cells)
    return jnp.maximum(0.0, 1.0 - distance)


def increment_block(cell_block, positions, increments, regress, centers, cells):
    slopes = jnp.dot(regress.T, cell_block, precision=HIGHEST_PREC)
    slopes = slopes * taper_weights(positions, centers, cells)
    return cell_block + jnp.dot(increments, slopes, precision=HIGHEST_PREC)


def sum_everywhere(partial_ens):
    axes = ("var", "mem")
    count = lax.axis_size("var") * lax.axis_size("mem")
    members, rays = partial_ens.shape
    pieces = partial_ens.reshape(members, count, rays // count).transpose(1, 0, 2)
    total = jnp.sum(lax.all_to_all(pieces, axes, split_axis=0, concat_axis=0, tiled=True), axis=0)
    copies = jnp.broadcast_to(total, pieces.shape)
    whole = lax.all_to_all(copies, axes, split_axis=0, concat_axis=0, tiled=True)
    return whole.transpose(1, 0, 2).reshape(members, rays)


def plain(ensemble, ray_cells, ray_weights, ray_centers, obs_values, obs_var):
    groups = lax.axis_size("mem")
    cell_count = ensemble.shape[1] // groups
    anchor = (lax.axis_index("var") * groups + lax.axis_index("mem")) * cell_count
    positions = (anchor + jnp.arange(cell_count, dtype=jnp.int32)).astype(jnp.float32)
    columns = lax.all_to_all(ensemble, "mem", split_axis=1, concat_axis=0, tiled=True)
    for batch_index in range(NBATCH):
        offsets = ray_cells[batch_index] - anchor
        inside = (offsets >= 0) & (offsets < cell_count)
        clipped = jnp.clip(offsets, 0, cell_count - 1)
        picked = jnp.take(columns, clipped.reshape(-1), axis=1)
        picked = picked.reshape(columns.shape[0], clipped.shape[0], clipped.shape[1])
        weights_here = jnp.where(inside, ray_weights[batch_index], 0.0)
        partial_ens = jnp.einsum("mjk,jk->mj", picked, weights_here, precision=HIGHEST_PREC)
        prior_ens = sum_everywhere(partial_ens)
        increments, regress = innovations(prior_ens, obs_values[batch_index], obs_var[batch_index])
        columns = increment_block(columns, positions, increments, regress, ray_centers[batch_index], cell_count)
    return lax.all_to_all(columns, "mem", split_axis=0, concat_axis=1, tiled=True)


def lanes_of(shape):
    return lax.broadcasted_iota(jnp.int32, shape, 1)


def squeeze_rows(packed, weight, mask):
    rows = packed.shape[0]
    lane = lanes_of(packed.shape)
    marks = mask.astype(BF16)
    upper = lax.broadcasted_iota(jnp.int32, (LANES, LANES), 0) < lanes_of((LANES, LANES))
    before = jnp.dot(marks, upper.astype(BF16), preferred_element_type=F32)
    count = jnp.dot(marks, jnp.ones((LANES, LANES), BF16), preferred_element_type=F32).astype(jnp.int32)
    gap = jnp.where(mask, lane - before.astype(jnp.int32), -1)
    for bit in range(7):
        step = 1 << bit
        moved_gap = pltpu.roll(gap, LANES - step, 1)
        take = (moved_gap >= 0) & ((moved_gap & step) != 0)
        keep = (gap >= 0) & ((gap & step) == 0)
        packed = jnp.where(take, pltpu.roll(packed, LANES - step, 1), packed)
        weight = jnp.where(take, pltpu.roll(weight, LANES - step, 1), weight)
        gap = jnp.where(take, moved_gap, jnp.where(keep, gap, -1))
    while rows > 8:
        rows //= 2
        first, second = count[:rows], count[rows:]
        p2, w2 = packed[rows:], weight[rows:]
        for bit in range(7):
            step = 1 << bit
            far = (first & step) != 0
            p2 = jnp.where(far, pltpu.roll(p2, step, 1), p2)
            w2 = jnp.where(far, pltpu.roll(w2, step, 1), w2)
        own = lanes_of(first.shape) < first
        packed = jnp.where(own, packed[:rows], p2)
        weight = jnp.where(own, weight[:rows], w2)
        count = first + second
    return packed, weight, count


def pick_kernel(n_var, n_mem, cells_in, weights_in, ens_ref, g_ref, tails_ref,
                cells_ref, weights_ref, ens_v, xt, graw, id_v, place_v, from_v, w_v, n_v, list_s, n_s, ens_sem, list_sem):
    members, span = ens_ref.shape
    nobs, kcells = cells_ref.shape[1:]
    rays_here = nobs // n_var
    load = pltpu.make_async_copy(ens_ref, ens_v, ens_sem)
    load.start()
    for batch in range(NBATCH):
        cells_ref[batch] = cells_in[batch].T
        weights_ref[batch] = weights_in[batch].T
    base = lax.axis_index("var") * span
    fold = LANES // kcells
    steps = rays_here // fold
    for part in range(n_var // 8):
        packs, weights = [], []
        for batch in range(NBATCH):
            for step in range(steps):
                rows = [pl.ds(part * 8 * rays_here + step + side * steps, 8, stride=rays_here) for side in range(fold)]
                place = jnp.concatenate([cells_ref[batch, row, :] for row in rows], axis=1) - base
                inside = (place >= 0) & (place < span)
                ray = batch * rays_here + step + lanes_of(place.shape) // kcells * steps
                packs.append(jnp.where(inside, jnp.bitwise_or(ray << 16, place & 0xFFFF), -1))
                weights.append(jnp.concatenate([weights_ref[batch, row, :] for row in rows], axis=1))
        packed = jnp.concatenate(packs, axis=0)
        packed, weight, count = squeeze_rows(packed, jnp.concatenate(weights, axis=0), packed >= 0)
        valid = lanes_of(count.shape) < count
        out_rows = pl.ds(part * 8, 8)
        place = jnp.where(valid, packed & 0xFFFF, 0)
        place_v[out_rows, :] = place
        from_v[out_rows, :] = ((place >> 9) << 7) | (place & 127)
        id_v[out_rows, :] = jnp.where(valid, packed >> 16, -1)
        w_v[out_rows, :] = jnp.where(valid, weight, 0.0)
        n_v[out_rows, :] = count
    to_list = pltpu.make_async_copy(from_v, list_s, list_sem.at[0])
    to_count = pltpu.make_async_copy(n_v, n_s, list_sem.at[1])
    to_list.start()
    to_count.start()
    load.wait()
    blank = jnp.zeros((32 - members, LANES), F32)
    half, step = span // n_mem // 2, 8 * LANES

    def fold_rows(index, carry):
        group, at = index // (half // step), lax.rem(index, half // step) * step
        ends = []
        for side in range(2):
            columns = pl.ds(pl.multiple_of((group * 2 + side) * half + at, LANES), step)
            ends.append(ens_v[FULL:, columns])
        tails_ref[group, :, pl.ds(pl.multiple_of(at, LANES), step)] = jnp.concatenate(ends, axis=0)
        return carry

    lax.fori_loop(0, n_mem * (half // step), fold_rows, 0)

    def turn(step, carry):
        for group in range(4):
            tiles = []
            for part in range(4):
                at = pl.ds(pl.multiple_of(((step * 4 + group) * 4 + part) * LANES, LANES), LANES)
                tiles += [ens_v[:, at], blank]
            to = pl.ds(pl.multiple_of((step * 4 + group) * LANES, LANES), LANES)
            xt[to, :] = jnp.concatenate(tiles, axis=0).T
        return carry

    lax.fori_loop(0, span // (16 * LANES), turn, 0)
    to_list.wait()
    to_count.wait()

    def gather_row(row, carry):
        def gather_some(block, inner):
            found = []
            for unit in range(16):
                found.append(xt[pl.ds(list_s[row, block * 16 + unit], 1), :])
            for unit in range(16):
                graw[pl.ds(row * LANES + block * 16 + unit, 1), :] = found[unit]
            return inner

        lax.fori_loop(0, (jnp.minimum(n_s[row, 0], LANES) + 15) // 16, gather_some, 0)
        return carry

    lax.fori_loop(0, n_var, gather_row, 0)
    sub = lax.broadcasted_iota(jnp.int32, (24, LANES), 0)
    for row in range(n_var):
        raw = graw[pl.ds(row * LANES, LANES), :].T
        place = place_v[pl.ds(row, 1), :]
        ids = id_v[pl.ds(row, 1), :]
        quarter = (place >> 7) & 3
        total = jnp.zeros((24, LANES), F32)
        for piece in range(4):
            total = jnp.where(quarter == piece, raw[32 * piece:32 * piece + 24, :], total)
        total = jnp.where(ids >= 0, total, 0.0) * w_v[pl.ds(row, 1), :]
        total = jnp.where(sub == members, ids.astype(F32), total)
        total = jnp.where(sub == members + 1, place.astype(F32), total)
        g_ref[row] = jnp.where(sub == members + 2, n_v[pl.ds(row, 1), :].astype(F32), total)


def pick(ensemble, ray_cells, ray_weights, n_var, n_mem):
    members, span = ensemble.shape
    vmem = pl.BlockSpec(memory_space=pltpu.VMEM)
    return pl.pallas_call(
        functools.partial(pick_kernel, n_var, n_mem),
        out_shape=(
            jax.ShapeDtypeStruct((n_var, 24, LANES), F32),
            jax.ShapeDtypeStruct((n_mem, 2 * (members - FULL), span // n_mem // 2), F32),
        ),
        in_specs=[vmem, vmem, pl.BlockSpec(memory_space=pl.ANY)],
        out_specs=(vmem, vmem),
        scratch_shapes=[
            pltpu.VMEM(ray_cells.shape, jnp.int32),
            pltpu.VMEM(ray_cells.shape, F32),
            pltpu.VMEM((members, span), F32),
            pltpu.VMEM((span // 4, LANES), F32),
            pltpu.VMEM((n_var * LANES, LANES), F32),
            pltpu.VMEM((n_var, LANES), jnp.int32),
            pltpu.VMEM((n_var, LANES), jnp.int32),
            pltpu.VMEM((n_var, LANES), jnp.int32),
            pltpu.VMEM((n_var, LANES), F32),
            pltpu.VMEM((n_var, LANES), jnp.int32),
            pltpu.SMEM((n_var, LANES), jnp.int32),
            pltpu.SMEM((n_var, LANES), jnp.int32),
            pltpu.SemaphoreType.DMA,
            pltpu.SemaphoreType.DMA((2,)),
        ],
        compiler_params=pltpu.CompilerParams(vmem_limit_bytes=48 << 20),
        cost_estimate=pl.CostEstimate(flops=1 << 30, bytes_accessed=64 << 20, transcendentals=0),
        name="pick",
    )(ray_cells.transpose(0, 2, 1), ray_weights.transpose(0, 2, 1), ensemble)


def split(x):
    high = x.astype(BF16)
    return high, (x - high.astype(F32)).astype(BF16)


def split_dot(a, b):
    a_high, a_low = split(a)
    b_high, b_low = split(b)
    total = jnp.dot(a_high, b_low, preferred_element_type=F32)
    total = total + jnp.dot(a_low, b_high, preferred_element_type=F32)
    return total + jnp.dot(a_high, b_high, preferred_element_type=F32)


def main_kernel(dims, ens_ref, tails_ref, g_ref, centers_ref, obs_ref, var_ref, early_refs, out_ref, full_ref,
                par_ref, xf, xtail, res, rtail, out_v, otail, xr, state, xb, agb, inc_v, reg_v, dpoly, dhi, dlo,
                mini_s, mini_r, fwd_s, fwd_r, tail_s, tail_r, own_sem, red_s, red_r, back_s, back_r, store_s):
    n_var, n_mem, members, cells, nobs, n_chunk = dims
    group = members // n_mem
    wide = 24 * n_mem
    sources = n_var // n_mem
    width = cells // n_chunk
    rays_here = nobs // n_var
    p, q = lax.axis_index("var"), lax.axis_index("mem")
    first = lax.rem(q + n_mem - p // sources, n_mem) * sources
    stays = p // sources == first // sources

    def var_peer(k):
        return {"var": lax.rem(p + k, n_var)}

    def mem_peer(k):
        return {"mem": lax.rem(q + k, n_mem)}

    barrier = pltpu.get_barrier_semaphore()

    def greet(k, carry):
        pl.semaphore_signal(barrier, inc=1, device_id=var_peer(k), device_id_type=MESH)
        return carry

    def greet_sender(k, carry):
        source, part = first + k // n_mem, lax.rem(k, n_mem)

        @pl.when((source != p) | (part != q))
        def _():
            pl.semaphore_signal(barrier, inc=1, device_id={"var": source, "mem": part}, device_id_type=MESH)

        return carry

    lax.fori_loop(0, n_var, greet_sender, 0)
    for k in range(1, n_mem):
        pl.semaphore_signal(barrier, inc=1, device_id=mem_peer(k), device_id_type=MESH)
    lax.fori_loop(1, n_var, greet, 0)
    lane = lanes_of((1, LANES))
    real_lane = (lax.rem(lane, 24) < group) & (lane < wide)
    block = p * n_mem + q
    rows = [centers_ref[...].astype(F32), obs_ref[...], var_ref[...]]
    rows.append(jnp.zeros((LANES - 3 * NBATCH, nobs), F32))
    par_ref[...] = jnp.concatenate(rows, axis=0).T
    pl.semaphore_wait(barrier, n_var - 1 + n_mem - 1 + n_var - stays.astype(jnp.int32))

    def send_mini(k, carry):
        there = lax.rem(p + k, n_var)
        taker = lax.rem(p // sources + there // sources, n_mem)

        @pl.when((k > 0) | jnp.logical_not(stays))
        def _():
            pltpu.make_async_remote_copy(
                src_ref=g_ref.at[there], dst_ref=xr.at[q, lax.rem(p, sources)],
                send_sem=mini_s, recv_sem=mini_r,
                device_id={"var": there, "mem": taker}, device_id_type=MESH).start()

        return carry

    lax.fori_loop(0, n_var, send_mini, 0)

    @pl.when(stays)
    def _():
        xr[q, lax.rem(p, sources)] = g_ref[p]

    def forward(k, chunk):
        there = lax.rem(q + k, n_mem)
        return pltpu.make_async_remote_copy(
            src_ref=ens_ref.at[pl.ds(0, FULL), pl.ds(pl.multiple_of(there * cells + chunk * width, LANES), width)],
            dst_ref=xf.at[q, :, pl.ds(pl.multiple_of(chunk * width, LANES), width)],
            send_sem=fwd_s.at[k, chunk], recv_sem=fwd_r.at[k, chunk],
            device_id=mem_peer(k), device_id_type=MESH)

    def start_forward(chunk, carry):
        for k in (2, 1, 3):
            forward(k, chunk).start()
        return carry

    def forward_tail(k, part):
        columns = pl.ds(part * (cells // 2 // TAIL_PARTS), cells // 2 // TAIL_PARTS)
        return pltpu.make_async_remote_copy(
            src_ref=tails_ref.at[lax.rem(q + k, n_mem), :, columns], dst_ref=xtail.at[q, :, columns],
            send_sem=tail_s.at[k, part], recv_sem=tail_r.at[k, part],
            device_id=mem_peer(k), device_id_type=MESH)

    paced = [EARLY - TAIL_PARTS]

    def pace(count):
        while count > 0 and paced[0] < EARLY:
            for k in (2, 1, 3):
                forward_tail(k, paced[0] - EARLY + TAIL_PARTS).start()
            paced[0] += 1
            count -= 1
        until = min(paced[0] + count, n_chunk)
        if until > paced[0]:
            lax.fori_loop(paced[0], until, start_forward, 0)
            paced[0] = until

    pace(PACE[0])
    mine = pl.ds(pl.multiple_of(q * cells, LANES), cells)
    landing = [
        pltpu.make_async_copy(ens_ref.at[pl.ds(0, FULL), mine], xf.at[q], own_sem.at[0]),
        pltpu.make_async_copy(tails_ref.at[q], xtail.at[q], own_sem.at[1]),
    ]
    for k in range(1, n_mem):
        there = xf.at[lax.rem(q + n_mem - k, n_mem), :, pl.ds(0, EARLY * width)]
        landing.append(pltpu.make_async_copy(early_refs[k - 1], there, own_sem.at[1 + k]))
    for copy in landing:
        copy.start()

    def wait_mini(count):
        landed = g_ref.at[pl.ds(0, count)]
        pltpu.make_async_remote_copy(
            src_ref=landed, dst_ref=landed, send_sem=mini_s, recv_sem=mini_r,
            device_id=mem_peer(1), device_id_type=MESH).wait()

    @pl.when(stays)
    def _():
        wait_mini(n_var - 1)

    @pl.when(jnp.logical_not(stays))
    def _():
        wait_mini(n_var)

    sub = lax.broadcasted_iota(jnp.int32, (24, LANES), 0)
    ids, places = [], []
    most = jnp.zeros((1, LANES), F32)
    for source in range(sources):
        for part in range(n_mem):
            tile = xr[part, source]
            state[pl.ds(part * 24, 24), pl.ds(source * LANES, LANES)] = jnp.where(sub < group, tile, 0.0)
        ids.append(xr[0, source, group:group + 1, :])
        most = jnp.maximum(most, xr[0, source, group + 2:group + 3, :])
        places.append(xr[0, source, group + 1:group + 2, :] + ((first + source) * (n_mem * cells)).astype(F32))
    id_row = jnp.concatenate(ids, axis=1)
    scale = 1.0 / (LRAD * cells)
    place_row = jnp.concatenate(places, axis=1) * scale
    own_ray = lax.broadcasted_iota(jnp.int32, (rays_here, 1), 0).astype(F32)

    def own_rows():
        return pl.ds(pl.multiple_of(p * rays_here, rays_here), rays_here)

    def across(batch, k):
        return pltpu.make_async_remote_copy(
            src_ref=xb.at[batch, q], dst_ref=xb.at[batch, q],
            send_sem=red_s.at[batch, k], recv_sem=red_r.at[batch, k],
            device_id=mem_peer(k), device_id_type=MESH)

    def start_reduce(batch):
        chosen = (id_row == own_ray + batch * rays_here).astype(BF16)
        high, low = split(state[...])
        total = jnp.zeros((rays_here, wide), F32)
        for piece in (low, high):
            total = total + lax.dot_general(chosen, piece, (((1,), (1,)), ((), ())), preferred_element_type=F32)
        over = jnp.broadcast_to((most > LANES).astype(F32), (rays_here, LANES))
        xb[batch, q] = jnp.concatenate([total, over[:, wide:]], axis=1)
        for k in (2, 1, 3):
            across(batch, k).start()

    def finish_reduce(batch):
        for k in (2, 1, 3):
            across(batch, k).wait()
        agb[batch, own_rows(), :] = jnp.sum(xb[batch], axis=0)
        mine = agb.at[batch, own_rows()]

        def send(k, carry):
            pltpu.make_async_remote_copy(
                src_ref=mine, dst_ref=mine,
                send_sem=red_s.at[batch, n_mem], recv_sem=red_r.at[batch, n_mem],
                device_id=var_peer(k), device_id_type=MESH).start()
            return carry

        lax.fori_loop(1, n_var, send, 0)
        pace(PACE[2])
        landed = agb.at[batch, pl.ds(0, nobs - rays_here)]
        pltpu.make_async_remote_copy(
            src_ref=landed, dst_ref=landed, send_sem=red_s.at[batch, n_mem], recv_sem=red_r.at[batch, n_mem],
            device_id=var_peer(1), device_id_type=MESH).wait()

    def innovate(batch):
        prior = agb[batch]
        obs = par_ref[:, NBATCH + batch:NBATCH + batch + 1]
        error_var = par_ref[:, 2 * NBATCH + batch:2 * NBATCH + batch + 1]
        mean = jnp.sum(jnp.where(real_lane, prior, 0.0), axis=1, keepdims=True) / members
        anomaly = jnp.where(real_lane, prior - mean, 0.0)
        variance = jnp.sum(anomaly * anomaly, axis=1, keepdims=True) / (members - 1) + EPSILON
        total_var = variance + error_var
        post_mean = (mean * error_var + obs * variance) / total_var
        shrink = jnp.sqrt(error_var / total_var)
        increments = jnp.where(real_lane, post_mean - mean + (shrink - 1.0) * anomaly, 0.0)
        inc_v[...] = increments.T
        reg_v[...] = anomaly / ((members - 1) * variance)

    def taper_at(batch, scaled):
        return 1.0 - jnp.abs(scaled - (par_ref[:, batch:batch + 1] + 0.5) * (cells * scale))

    def update_state(batch):
        slopes = split_dot(reg_v[:, 0:wide], state[...])
        slopes = slopes * jnp.maximum(taper_at(batch, place_row), 0.0)
        state[...] += split_dot(inc_v[0:wide, :], slopes)

    def compose(batch):
        for half in range(2):
            start = (block * cells + half * (cells // 2)).astype(F32) * scale
            near, far = taper_at(batch, start), taper_at(batch, start + (cells // 2) * scale)
            inside = near + far > 0.0
            alpha = jnp.where(inside, near, 0.0)
            beta = jnp.where(inside, far - near, 0.0)
            regress = reg_v[...]
            both = jnp.concatenate([regress * alpha, regress * beta], axis=1)
            ab = split_dot(inc_v[0:wide, :], both)
            a, b = ab[:, :LANES], ab[:, LANES:]
            if batch == 0:
                dpoly[half, 0], dpoly[half, 1] = a, b
                continue
            old = jnp.concatenate([dpoly[half, k] for k in range(batch + 1)], axis=1)
            left = jnp.concatenate([a[:, 0:wide], b[:, 0:wide]], axis=0)
            made = split_dot(left, old)
            for k in range(batch + 2):
                total = a if k == 0 else b if k == 1 else jnp.zeros_like(a)
                if k <= batch:
                    total = total + dpoly[half, k] + made[:wide, k * LANES:(k + 1) * LANES]
                if k >= 1:
                    total = total + made[wide:, (k - 1) * LANES:k * LANES]
                dpoly[half, k] = total

    start_reduce(0)
    for batch in range(NBATCH):
        pace(PACE[1])
        if batch:
            compose(batch - 1)
        finish_reduce(batch)
        pace(PACE[3])
        innovate(batch)
        if batch + 1 < NBATCH:
            update_state(batch)
            start_reduce(batch + 1)
    pace(n_chunk)
    compose(NBATCH - 1)

    terms = NBATCH + 1
    for half in range(2):
        for k in range(terms):
            high, low = split(dpoly[half, k][:, 0:wide])
            dhi[half, pl.ds(k * wide, wide), :] = high
            dlo[half, pl.ds(k * wide, wide), :] = low

    full_ref[...] = jnp.max(agb[0], axis=0, keepdims=True)
    for copy in landing:
        copy.wait()
    for k in (2, 1, 3):
        for part in range(TAIL_PARTS):
            forward_tail(k, part).wait()

    pairs = n_chunk // 2
    rest = group - FULL

    def columns_of(block_index, pair, side):
        return pl.ds(pl.multiple_of(block_index * cells + (side * pairs + pair) * width, LANES), width)

    def back(k, pair):
        there = lax.rem(q + k, n_mem)
        tail = pl.ds(pl.multiple_of(pair * width, LANES), width)
        ends = [(res.at[there, :, columns_of(0, pair, side)], out_v.at[pl.ds(0, FULL), columns_of(q, pair, side)])
                for side in range(2)]
        ends.append((rtail.at[there, :, tail], otail.at[q, :, tail]))
        if k == 0:
            return [pltpu.make_async_copy(a, b, back_r.at[0, pair, n]) for n, (a, b) in enumerate(ends)]
        return [pltpu.make_async_remote_copy(
            src_ref=a, dst_ref=b, send_sem=back_s.at[k, pair, n], recv_sem=back_r.at[k, pair, n],
            device_id=mem_peer(k), device_id_type=MESH) for n, (a, b) in enumerate(ends)]

    def store(source, pair, side):
        columns = columns_of(source, pair, side)
        return pltpu.make_async_copy(out_v.at[:, columns], out_ref.at[:, columns], store_s.at[source])

    def drain(pair):
        tail = pl.ds(pl.multiple_of(pair * width, LANES), width)
        for k in (0, 1, 3, 2):
            source = lax.rem(q + n_mem - k, n_mem)
            for copy in back(k, pair):
                copy.wait()
            folded = otail[source, :, tail]
            for side in range(2):
                out_v[FULL:, columns_of(source, pair, side)] = folded[side * rest:(side + 1) * rest]
                store(source, pair, side).start()

    pad = jnp.zeros((24 - group, width), F32)

    def apply(pair, carry):
        tail = pl.ds(pl.multiple_of(pair * width, LANES), width)
        for side in range(2):
            chunk = side * pairs + pair

            @pl.when(chunk >= EARLY)
            def _():
                for k in (2, 1, 3):
                    forward(k, chunk).wait()

            at = pl.ds(pl.multiple_of(chunk * width, LANES), width)
            pieces = []
            for i in range(n_mem):
                pieces += [xf[i, :, at], xtail[i, side * rest:(side + 1) * rest, tail], pad]
            x = jnp.concatenate(pieces, axis=0)
            high, low = split(x)
            big, small = dhi[side], dlo[side]
            y = jnp.dot(big, high, preferred_element_type=F32)
            y = y + jnp.dot(big, low, preferred_element_type=F32)
            y = y + jnp.dot(small, high, preferred_element_type=F32)
            t = (lanes_of((1, width)) + pair * width).astype(F32) * (2.0 / cells)
            total = y[(terms - 1) * wide:]
            for k in range(terms - 2, -1, -1):
                total = y[k * wide:(k + 1) * wide] + t * total
            total = x + total
            for i in range(n_mem):
                res[i, :, at] = total[24 * i:24 * i + FULL]
                rtail[i, side * rest:(side + 1) * rest, tail] = total[24 * i + FULL:24 * i + group]
        for k in (2, 1, 3, 0):
            for copy in back(k, pair):
                copy.start()

        @pl.when(pair >= LAG)
        def _():
            drain(pair - LAG)

        return carry

    lax.fori_loop(0, pairs, apply, 0)

    def drain_rest(pair, carry):
        drain(pair)
        return carry

    lax.fori_loop(pairs - LAG, pairs, drain_rest, 0)
    for source in range(n_mem):
        columns = pl.ds(source * cells, cells)
        pltpu.make_async_copy(out_v.at[:, columns], out_ref.at[:, columns], store_s.at[source]).wait()


def assimilate(ensemble, tails, picked, ray_centers, obs_values, obs_var, early, n_var, n_mem):
    group, span = ensemble.shape
    cells = span // n_mem
    nobs = ray_centers.shape[1]
    wide = 24 * n_mem
    slots = n_var // n_mem * LANES
    rays_here = nobs // n_var
    vmem = pl.BlockSpec(memory_space=pltpu.VMEM)
    anywhere = pl.BlockSpec(memory_space=pl.ANY)
    dma = pltpu.SemaphoreType.DMA
    dims = (n_var, n_mem, group * n_mem, cells, nobs, N_CHUNK)
    return pl.pallas_call(
        functools.partial(main_kernel, dims),
        out_shape=(jax.ShapeDtypeStruct((group, span), F32), jax.ShapeDtypeStruct((1, LANES), F32)),
        in_specs=[anywhere, anywhere, vmem, vmem, vmem, vmem, [anywhere] * len(early)],
        out_specs=(anywhere, vmem),
        scratch_shapes=[
            pltpu.VMEM((nobs, LANES), F32),
            pltpu.VMEM((n_mem, FULL, cells), F32),
            pltpu.VMEM(tails.shape, F32),
            pltpu.VMEM((n_mem, FULL, cells), F32),
            pltpu.VMEM(tails.shape, F32),
            pltpu.VMEM((group, span), F32),
            pltpu.VMEM(tails.shape, F32),
            pltpu.VMEM((n_mem, n_var // n_mem, 24, LANES), F32),
            pltpu.VMEM((wide, slots), F32),
            pltpu.VMEM((NBATCH, n_mem, rays_here, LANES), F32),
            pltpu.VMEM((NBATCH, nobs, LANES), F32),
            pltpu.VMEM((LANES, nobs), F32),
            pltpu.VMEM((nobs, LANES), F32),
            pltpu.VMEM((2, NBATCH + 1, wide, LANES), F32),
            pltpu.VMEM((2, (NBATCH + 1) * wide, wide), BF16),
            pltpu.VMEM((2, (NBATCH + 1) * wide, wide), BF16),
            dma, dma,
            dma((n_mem, N_CHUNK)), dma((n_mem, N_CHUNK)),
            dma((n_mem, TAIL_PARTS)), dma((n_mem, TAIL_PARTS)),
            dma((1 + n_mem,)),
            dma((NBATCH, n_mem + 1)), dma((NBATCH, n_mem + 1)),
            dma((n_mem, N_CHUNK // 2, 3)), dma((n_mem, N_CHUNK // 2, 3)),
            dma((n_mem,)),
        ],
        compiler_params=pltpu.CompilerParams(collective_id=1, has_side_effects=True, vmem_limit_bytes=48 << 20),
        name="assimilate",
    )(ensemble, tails, picked, ray_centers, obs_values, obs_var, early)


def first_columns(ensemble, n_mem):
    group, span = ensemble.shape
    cells = span // n_mem
    q = lax.axis_index("mem")
    arrived = []
    for k in range(1, n_mem):
        start = lax.rem(q + k, n_mem) * cells
        piece = lax.dynamic_slice(ensemble, (0, start), (FULL, EARLY * (cells // N_CHUNK)))
        arrived.append(lax.ppermute(piece, "mem", [(i, (i + k) % n_mem) for i in range(n_mem)]))
    return arrived


def fast(ensemble, ray_cells, ray_weights, ray_centers, obs_values, obs_var):
    n_var, n_mem = lax.axis_size("var"), lax.axis_size("mem")
    early = first_columns(ensemble, n_mem)
    picked, tails = pick(ensemble, ray_cells, ray_weights, n_var, n_mem)
    return assimilate(ensemble, tails, picked, ray_centers, obs_values, obs_var, early, n_var, n_mem)


def shards(*arrays):
    made, full = fast(*arrays)
    return lax.cond(full[0, LANES - 1] < 0.5, lambda made, *rest: made, lambda made, *rest: plain(*rest), made, *arrays)


def solution(mesh):
    placed = (P("mem", "var"), P(), P(), P(), P(), P())
    return jax.shard_map(
        shards, mesh=mesh, in_specs=placed, out_specs=P("mem", "var"), check_vma=False
    )
```
